32 devices in a mesh: dp: 8 (over y, x, core), seq: 4 (over z).
Axes of the slice: x: 2, y: 2, z: 4, core: 2. Of those that a mesh axis runs over, the one named last changes fastest.
Arguments:
- frames_in: bfloat16 [2, 16, 16, 208, 768], P(None, 'dp', 'seq'), may hold values from -6 to 6
- qkv_spatial: bfloat16 [768, 2304], P(('dp', 'seq')), may hold values from -0.21875 to 0.21875
- out_spatial: bfloat16 [768, 768], P(('dp', 'seq')), may hold values from -0.875 to 0.875
- qkv_temporal: bfloat16 [768, 2304], P(('dp', 'seq')), may hold values from -0.21875 to 0.21875
- out_temporal: bfloat16 [768, 768], P(('dp', 'seq')), may hold values from -0.4375 to 0.4375
- mlp_in: bfloat16 [768, 3072], P(('dp', 'seq')), may hold values from -0.21875 to 0.21875
- mlp_out: bfloat16 [3072, 768], P(('dp', 'seq')), may hold values from -0.109375 to 0.109375
- gains: bfloat16 [768, 3], P(('dp', 'seq')), may hold values from 0.099609375 to 1.8984375
- place_mask: int32 [208], replicated, may hold values from 0 to 1, as said below
- cotangent: bfloat16 [2, 16, 16, 208, 768], P(None, 'dp', 'seq'), may hold values from -6 to 6
Outputs:
- frames_out: bfloat16 [2, 16, 16, 208, 768], P(None, 'dp', 'seq')
- frames_grad: float32 [2, 16, 16, 208, 768], P(None, 'dp', 'seq')
- qkv_spatial_grad: float32 [768, 2304], P(('dp', 'seq'))
- out_spatial_grad: float32 [768, 768], P(('dp', 'seq'))
- qkv_temporal_grad: float32 [768, 2304], P(('dp', 'seq'))
- out_temporal_grad: float32 [768, 768], P(('dp', 'seq'))
- mlp_in_grad: float32 [768, 3072], P(('dp', 'seq'))
- mlp_out_grad: float32 [3072, 768], P(('dp', 'seq'))
- gains_grad: float32 [768, 3], P(('dp', 'seq'))
The draws below stay inside these ranges and needn't reach their ends.
Inputs may be any that keep to these rules, and one draw needn't show every extreme that they name: `place_mask`: exactly 196 of the 208 entries are 1; which slots are padding varies with the seed.
All inputs are finite; a program needn't handle non-finite values.
Results may differ from the reference program's by a relative error of at most 0.028.
Values may be sent and summed in bfloat16 or wider, within the bound.
No kernel may reach another device: no remote copies, remote signals or barrier semaphores. Data moves between devices by JAX's collectives and lax.ppermute only.
A program may use at most 576 MiB of HBM per device.

```python
import jax
import jax.numpy as jnp
from jax import lax

D = 768
HEADS = 12
HEAD_DIM = 64
FF = 3072
SLOTS = 208
PLACES = 196
MB = 2
FRAMES = 16
CLIPS = 16


def draw_place_mask(key, part):
    key = jax.random.fold_in(key, 7)
    shuffled = jax.random.permutation(key, SLOTS)
    return (shuffled < PLACES).astype(jnp.int32)


def shard_levels(stream_key, extent, cuts, low, top_value):
    factor_of, own = 1.0, jax.random.fold_in(stream_key, 6)
    for axis_at, parts in cuts:
        draws = jnp.exp(jax.random.uniform(jax.random.fold_in(own, axis_at), (parts,), jnp.float32, low / len(cuts), top_value / len(cuts)))
        factor_of = factor_of * jnp.repeat(draws, extent[axis_at] // parts).reshape([-1 if axis == axis_at else 1 for axis in range(len(extent))])
    return factor_of


def centred(key, shape, scale, limit, shards=(), kind=jnp.bfloat16):
    entries = scale * jax.random.normal(key, shape, jnp.float32)
    if shards:
        entries = entries * shard_levels(key, shape, shards, -0.22, 0.18)
    return jnp.clip(entries, -limit, limit).astype(kind)


def setup_inputs(seed: int = 0) -> dict:
    key_list = jax.random.split(jax.random.key(seed), 11)
    frames_in = centred(key_list[0], (MB, CLIPS, FRAMES, SLOTS, D), 1.0, 6.0, ((1, 8), (2, 4)))
    qkv_spatial = centred(key_list[1], (D, 3 * D), D ** -0.5, 0.21875, ((0, 32),))
    out_spatial = centred(key_list[2], (D, D), (D // 16) ** -0.5, 0.875, ((0, 32),))
    qkv_temporal = centred(key_list[3], (D, 3 * D), D ** -0.5, 0.21875, ((0, 32),))
    out_temporal = centred(key_list[4], (D, D), (D // 4) ** -0.5, 0.4375, ((0, 32),))
    mlp_in = centred(key_list[5], (D, FF), D ** -0.5, 0.21875, ((0, 32),))
    mlp_out = centred(key_list[6], (FF, D), FF ** -0.5, 0.109375, ((0, 32),))
    gains = jnp.clip(1.0 + 0.18 * jax.random.normal(key_list[7], (D, 3), jnp.float32), 0.099609375, 1.8984375).astype(jnp.bfloat16)
    place_mask = draw_place_mask(jax.random.fold_in(key_list[10], 71), 0)
    cotangent = centred(key_list[9], (MB, CLIPS, FRAMES, SLOTS, D), 1.0, 6.0, ((1, 8), (2, 4)))
    return {"frames_in": frames_in, "qkv_spatial": qkv_spatial, "out_spatial": out_spatial, "qkv_temporal": qkv_temporal, "out_temporal": out_temporal, "mlp_in": mlp_in, "mlp_out": mlp_out, "gains": gains, "place_mask": place_mask, "cotangent": cotangent}


@jax.custom_vjp
def low(v):
    return lax.optimization_barrier(v.astype(jnp.bfloat16)).astype(jnp.float32)

@jax.custom_vjp
def low_back(v):
    return v

def low_keep(v):
    return (low(v), None)

def low_pass(kept, grad):
    return (grad,)

def back_keep(v):
    return (v, None)

def back_low(kept, grad):
    return (low(grad),)
low.defvjp(low_keep, low_pass)
low_back.defvjp(back_keep, back_low)
highest = lax.Precision.HIGHEST

def both_round(values_in):
    return low_back(low(values_in))

def layer_norm(values_in, norm_gain):
    centered = values_in - lax.optimization_barrier(jnp.mean(values_in, axis=-1, keepdims=True))
    spread = lax.optimization_barrier(jnp.mean(centered * centered, axis=-1, keepdims=True))
    return centered * lax.rsqrt(spread + 1e-06) * norm_gain

def attend(query_rows, key_rows, value_rows, allowed):
    scores = jnp.einsum('bqhe,bkhe->bhqk', query_rows, key_rows, precision=highest) * HEAD_DIM ** (-0.5)
    scores = low_back(scores)
    scores = jnp.where(allowed, scores, -1000000000.0)
    weights = low(jax.nn.softmax(scores, axis=-1))
    return jnp.einsum('bhqk,bkhe->bqhe', weights, value_rows, precision=highest)

def clip_layer(inputs, qkv_spatial, out_spatial, qkv_temporal, out_temporal, mlp_in, mlp_out, gains, allowed, keep_rows):
    frame_count, slot_count = (inputs.shape[0], inputs.shape[1])
    normed = low(layer_norm(inputs, gains[:, 0]))
    mixed = both_round(jnp.dot(normed, qkv_spatial, precision=highest))
    mixed = mixed.reshape(frame_count, slot_count, 3, HEADS, HEAD_DIM)
    attended = attend(mixed[:, :, 0], mixed[:, :, 1], mixed[:, :, 2], allowed)
    attended = both_round(attended.reshape(frame_count, slot_count, D))
    after_space = inputs + low_back(jnp.dot(attended, out_spatial, precision=highest))
    across = jnp.swapaxes(after_space, 0, 1)
    normed = low(layer_norm(across, gains[:, 1]))
    mixed = both_round(jnp.dot(normed, qkv_temporal, precision=highest))
    mixed = mixed.reshape(slot_count, frame_count, 3, HEADS, HEAD_DIM)
    attended = attend(mixed[:, :, 0], mixed[:, :, 1], mixed[:, :, 2], True)
    attended = both_round(attended.reshape(slot_count, frame_count, D))
    second = across + low_back(jnp.dot(attended, out_temporal, precision=highest))
    second = jnp.swapaxes(second, 0, 1)
    normed = low(layer_norm(second, gains[:, 2]))
    hidden = low_back(jnp.dot(normed, mlp_in, precision=highest))
    active = low(jax.nn.gelu(hidden))
    result = second + low_back(jnp.dot(active, mlp_out, precision=highest))
    return result * keep_rows

def reference(frames_in, qkv_spatial, out_spatial, qkv_temporal, out_temporal, mlp_in, mlp_out, gains, place_mask, cotangent):
    params = (qkv_spatial.astype(jnp.float32), out_spatial.astype(jnp.float32), qkv_temporal.astype(jnp.float32), out_temporal.astype(jnp.float32), mlp_in.astype(jnp.float32), mlp_out.astype(jnp.float32), gains.astype(jnp.float32))
    allowed = (place_mask > 0)[None, None, None, :]
    keep_rows = place_mask.astype(jnp.float32)[None, :, None]
    clips_in = frames_in.astype(jnp.float32).reshape(-1, FRAMES, SLOTS, D)
    seeds = cotangent.astype(jnp.float32).reshape(-1, FRAMES, SLOTS, D)

    def forward(clip, w_one, w_two, w_three, w_four, w_five, w_six, w_seven):
        return clip_layer(clip, w_one, w_two, w_three, w_four, w_five, w_six, w_seven, allowed, keep_rows)

    def one_clip(totals, paired):
        clip, upstream = paired
        result, pullback = jax.vjp(forward, clip, *params)
        grads = pullback(upstream)
        totals = tuple((total + grad for total, grad in zip(totals, grads[1:])))
        return (totals, (result.astype(jnp.bfloat16), grads[0]))
    zeros = tuple((jnp.zeros_like(weight) for weight in params))
    totals, (outputs, input_grads) = lax.scan(one_clip, zeros, (clips_in, seeds))
    full_shape = frames_in.shape
    return (outputs.reshape(full_shape), input_grads.reshape(full_shape), totals[0], totals[1], totals[2], totals[3], totals[4], totals[5], totals[6])
```

```python
import functools

import jax
import jax.numpy as jnp
from jax import lax
from jax.experimental import pallas as pl
from jax.experimental.pallas import tpu as pltpu
from jax.sharding import PartitionSpec as P

HEAD_DIM = 64
PAIR = 2 * HEAD_DIM
QUAD = 4 * HEAD_DIM
EPSILON = 1e-06
LOW = jnp.bfloat16
F32 = jnp.float32
VMEM_LIMIT = 60 * 1024 * 1024
GELU_A = 0.7978845608028654
GELU_B = 0.044715


def dot(a, b):
    return lax.dot_general(a, b, (((1,), (0,)), ((), ())), preferred_element_type=F32)


def dot_nt(a, b):
    return lax.dot_general(a, b, (((1,), (1,)), ((), ())), preferred_element_type=F32)


def dot_tn(a, b):
    return lax.dot_general(a, b, (((0,), (0,)), ((), ())), preferred_element_type=F32)


def row_block(rows, most=512):
    for parts in range(1, rows + 1):
        if rows % parts == 0 and rows // parts <= most and (rows // parts) % 16 == 0:
            return rows // parts
    return rows


def loop_rows(total, size, body):
    @pl.loop(0, total // size)
    def _(step):
        body(pl.ds(pl.multiple_of(step * size, size), size))


def normalise(v):
    centered = v - jnp.mean(v, axis=-1, keepdims=True)
    spread = jnp.mean(centered * centered, axis=-1, keepdims=True)
    inverse = lax.rsqrt(spread + EPSILON)
    return centered * inverse, inverse


def norm_back(v, gain, grad):
    n, inverse = normalise(v)
    scaled = grad * gain
    back = scaled - jnp.mean(scaled, axis=-1, keepdims=True) - n * jnp.mean(scaled * n, axis=-1, keepdims=True)
    return back * inverse, jnp.sum(grad * n, axis=0, keepdims=True)


def half_masks(kind):
    lane = lax.broadcasted_iota(jnp.int32, (1, PAIR), 1)
    first = (lane < HEAD_DIM).astype(F32)
    return first.astype(kind), (1.0 - first).astype(kind)


def spread_pair(v):
    first, second = half_masks(v.dtype)
    return jnp.concatenate([v * first, v * second], axis=0)


def join_pair(v):
    tile = v.shape[0] // 2
    first, second = half_masks(v.dtype)
    return v[:tile] * first + v[tile:] * second


def attend_fwd(tile, x_ref, gain_ref, bias_ref, wq_ref, wk_ref, wv_ref, wo_ref,
               out_ref, n_ref, q_ref, k_ref, v_ref, p_ref, att_ref, acc_ref):
    step, steps = pl.program_id(0), pl.num_programs(0)
    rows = x_ref.shape[0]
    rb = row_block(rows)
    small = row_block(rows, 64)

    @pl.when(step == 0)
    def _():
        def body(at):
            x = x_ref[at, :].astype(F32)
            n_ref[at, :] = (normalise(x)[0] * gain_ref[...]).astype(LOW)
            acc_ref[at, :] = x
        loop_rows(rows, small, body)

    def project(at):
        n = n_ref[at, :]
        q_ref[at, :] = (dot(n, wq_ref[...]).astype(LOW) * (HEAD_DIM ** -0.5)).astype(LOW)
        k_ref[at, :] = dot(n, wk_ref[...]).astype(LOW)
        v_ref[at, :] = dot(n, wv_ref[...]).astype(LOW)
    loop_rows(rows, rb, project)

    @pl.loop(0, rows // tile)
    def _(t):
        at = pl.ds(pl.multiple_of(t * tile, tile), tile)
        for pair in range(2):
            cols = pl.ds(pair * PAIR, PAIR)
            qs = spread_pair(q_ref[at, cols])
            s = dot_nt(qs, k_ref[at, cols]) + bias_ref[...]
            e = jnp.exp(s - jnp.max(s, axis=-1, keepdims=True))
            p = (e * (1.0 / jnp.sum(e, axis=-1, keepdims=True))).astype(LOW)
            p_ref[0, pl.ds(pl.multiple_of((t * 2 + pair) * 2 * tile, 2 * tile), 2 * tile), :] = p
            att_ref[at, cols] = join_pair(dot(p, v_ref[at, cols])).astype(LOW)

    def project_out(at):
        acc_ref[at, :] += dot(att_ref[at, :], wo_ref[...])
    loop_rows(rows, rb, project_out)

    @pl.when(step == steps - 1)
    def _():
        out_ref[...] = acc_ref[...].astype(out_ref.dtype)


def attend_bwd(tile, prior, g_ref, x_ref, gain_ref, n_ref, q_ref, k_ref, v_ref, p_ref, att_ref,
               wq_ref, wk_ref, wv_ref, wo_ref, *rest):
    if prior:
        old_ref, oldo_ref, oldg_ref, gx_ref, dw_ref, dwo_ref, dgain_ref = rest[:7]
        rest = rest[7:]
    else:
        gx_ref, dw_ref, dwo_ref, dgain_ref = rest[:4]
        rest = rest[4:]
    low_ref, nt_ref, do_ref, dq_ref, dk_ref, dv_ref, acc_ref = rest
    step, steps = pl.program_id(0), pl.num_programs(0)
    rows, width = x_ref.shape
    rb = row_block(rows)
    small = row_block(rows, 64)

    @pl.when(step == 0)
    def _():
        low_ref[...] = g_ref[...].astype(LOW)
        nt_ref[...] = n_ref[...].T

    def back_out(at):
        do_ref[at, :] = dot_nt(low_ref[at, :], wo_ref[...]).astype(LOW)
    loop_rows(rows, rb, back_out)
    total = dot_tn(att_ref[...], low_ref[...])
    if prior:
        total += oldo_ref[...]
    dwo_ref[...] = total.astype(dwo_ref.dtype)

    @pl.loop(0, rows // tile)
    def _(t):
        at = pl.ds(pl.multiple_of(t * tile, tile), tile)
        for pair in range(2):
            cols = pl.ds(pair * PAIR, PAIR)
            dos = spread_pair(do_ref[at, cols])
            att = att_ref[at, cols].astype(F32)
            inner = jnp.sum(dos.astype(F32) * jnp.concatenate([att, att], axis=0), axis=-1, keepdims=True)
            p = p_ref[0, pl.ds(pl.multiple_of((t * 2 + pair) * 2 * tile, 2 * tile), 2 * tile), :]
            ds = (p.astype(F32) * (dot_nt(dos, v_ref[at, cols]) - inner)).astype(LOW)
            dq_ref[at, cols] = (join_pair(dot(ds, k_ref[at, cols])) * (HEAD_DIM ** -0.5)).astype(LOW)
            dk_ref[at, cols] = dot_tn(ds, spread_pair(q_ref[at, cols])).astype(LOW)
            dv_ref[at, cols] = dot_tn(p, dos).astype(LOW)

    def back_in(at):
        part = dot_nt(dq_ref[at, :], wq_ref[...]) + dot_nt(dk_ref[at, :], wk_ref[...]) + dot_nt(dv_ref[at, :], wv_ref[...])

        @pl.when(step == 0)
        def _():
            acc_ref[at, :] = part

        @pl.when(step != 0)
        def _():
            acc_ref[at, :] += part
    loop_rows(rows, rb, back_in)
    for at, grad_ref in enumerate((dq_ref, dk_ref, dv_ref)):
        total = dot(nt_ref[...], grad_ref[...])
        if prior:
            total += old_ref[at]
        dw_ref[at] = total.astype(dw_ref.dtype)

    @pl.when(step == steps - 1)
    def _():
        if prior:
            dgain_ref[...] = oldg_ref[...]
        else:
            dgain_ref[...] = jnp.zeros_like(dgain_ref)

        def body(at):
            back, gains = norm_back(x_ref[at, :].astype(F32), gain_ref[...], acc_ref[at, :])
            dgain_ref[...] += gains
            gx_ref[at, :] = (g_ref[at, :].astype(F32) + back).astype(gx_ref.dtype)
        loop_rows(rows, small, body)


def mlp_both(prior, second_ref, cot_ref, keep_ref, gain_ref, w1_ref, w2_ref, *rest):
    if prior:
        old1_ref, old2_ref, oldg_ref, out_ref, grad_ref, dw1_ref, dw2_ref, dgain_ref = rest[:8]
        rest = rest[8:]
    else:
        out_ref, grad_ref, dw1_ref, dw2_ref, dgain_ref = rest[:5]
        rest = rest[5:]
    n_ref, nt_ref, up_ref, sum_ref, acc_ref, act_ref, gh_ref = rest
    step, steps = pl.program_id(0), pl.num_programs(0)
    rows = second_ref.shape[0]
    rb = row_block(rows, 256)
    small = row_block(rows, 64)

    @pl.when(step == 0)
    def _():
        def body(at):
            v = second_ref[at, :]
            n_ref[at, :] = (normalise(v)[0] * gain_ref[...]).astype(LOW)
            up_ref[at, :] = (cot_ref[at, :].astype(F32) * keep_ref[at, :]).astype(LOW)
            sum_ref[at, :] = v
            acc_ref[at, :] = jnp.zeros_like(v)
        loop_rows(rows, small, body)
        nt_ref[...] = n_ref[...].T

    def body(at):
        h = dot(n_ref[at, :], w1_ref[...])
        ga = dot_nt(up_ref[at, :], w2_ref[...])
        square = h * h
        t = jnp.tanh(GELU_A * h * (1.0 + GELU_B * square))
        half = 0.5 + 0.5 * t
        act = (h * half).astype(LOW)
        slope = half + h * (0.5 - 0.5 * t * t) * (GELU_A + (3.0 * GELU_A * GELU_B) * square)
        gh = (ga * slope).astype(LOW)
        act_ref[at, :] = act
        gh_ref[at, :] = gh
        sum_ref[at, :] += dot(act, w2_ref[...])
        acc_ref[at, :] += dot_nt(gh, w1_ref[...])
    loop_rows(rows, rb, body)
    total = dot(nt_ref[...], gh_ref[...])
    if prior:
        total += old1_ref[...]
    dw1_ref[...] = total.astype(dw1_ref.dtype)
    total = dot_tn(act_ref[...], up_ref[...])
    if prior:
        total += old2_ref[...]
    dw2_ref[...] = total.astype(dw2_ref.dtype)

    @pl.when(step == steps - 1)
    def _():
        if prior:
            dgain_ref[...] = oldg_ref[...]
        else:
            dgain_ref[...] = jnp.zeros_like(dgain_ref)

        def last(at):
            out_ref[at, :] = (keep_ref[at, :] * sum_ref[at, :]).astype(LOW)
            back, gains = norm_back(second_ref[at, :], gain_ref[...], acc_ref[at, :])
            dgain_ref[...] += gains
            grad_ref[at, :] = up_ref[at, :].astype(F32) + back
        loop_rows(rows, small, last)


def whole(shape):
    return pl.BlockSpec(shape, lambda i: (0,) * len(shape), pipeline_mode=pl.Buffered(1))


def fixed(shape):
    return pl.BlockSpec(shape, lambda i: (0,) * len(shape))


def params():
    return pltpu.CompilerParams(dimension_semantics=("arbitrary",), vmem_limit_bytes=VMEM_LIMIT)


def spec_cols(shape, offset=0):
    return pl.BlockSpec(shape, lambda i, o=offset: (0, o + i))


def spec_rows(shape, offset=0):
    return pl.BlockSpec(shape, lambda i, o=offset: (o + i, 0))


def weight_specs(width, quads):
    return [spec_cols((width, QUAD), at * quads) for at in range(3)] + [spec_rows((QUAD, width))]


def run_attend_fwd(x, gain, bias, qkv, out_weight, tile, out_type):
    rows, width = x.shape
    quads = width // QUAD
    tiles = rows // tile
    probs_rows = tiles * 4 * tile
    low = jax.ShapeDtypeStruct((rows, width), LOW)
    cost = pl.CostEstimate(flops=2 * rows * width * (4 * width + 8 * tile), bytes_accessed=rows * width * 14 + 8 * width * width + 2 * rows * tile * (width // HEAD_DIM), transcendentals=rows * tile * (width // HEAD_DIM))
    return pl.pallas_call(
        functools.partial(attend_fwd, tile),
        grid=(quads,),
        in_specs=[whole((rows, width)), whole((1, width)), whole(bias.shape)] + weight_specs(width, quads),
        out_specs=[fixed((rows, width)), fixed((rows, width))] + [spec_cols((rows, QUAD))] * 3
        + [pl.BlockSpec((1, probs_rows, tile), lambda i: (i, 0, 0)), spec_cols((rows, QUAD))],
        out_shape=[jax.ShapeDtypeStruct((rows, width), out_type), low, low, low, low,
                   jax.ShapeDtypeStruct((quads, probs_rows, tile), LOW), low],
        scratch_shapes=[pltpu.VMEM((rows, width), F32)],
        compiler_params=params(),
        cost_estimate=cost,
    )(x, gain, bias, qkv, qkv, qkv, out_weight)


def run_attend_bwd(grad, x, gain, saved, qkv, out_weight, tile, out_type, old=None, weight_type=F32):
    n, q, k, v, probs, att = saved
    rows, width = x.shape
    quads = width // QUAD
    probs_rows = probs.shape[1]
    cost = pl.CostEstimate(flops=2 * rows * width * (8 * width + 20 * tile), bytes_accessed=rows * width * 20 + 24 * width * width + 2 * rows * tile * (width // HEAD_DIM), transcendentals=0)
    weight_out = [pl.BlockSpec((3, width, QUAD), lambda i: (0, 0, i)), spec_rows((QUAD, width)), fixed((1, width))]
    extra = [] if old is None else list(old)
    return pl.pallas_call(
        functools.partial(attend_bwd, tile, old is not None),
        grid=(quads,),
        in_specs=[whole((rows, width)), whole((rows, width)), whole((1, width)), whole((rows, width))]
        + [spec_cols((rows, QUAD))] * 3 + [pl.BlockSpec((1, probs_rows, tile), lambda i: (i, 0, 0)), spec_cols((rows, QUAD))]
        + weight_specs(width, quads) + (weight_out if extra else []),
        out_specs=[fixed((rows, width))] + weight_out,
        out_shape=[jax.ShapeDtypeStruct((rows, width), out_type), jax.ShapeDtypeStruct((3, width, width), weight_type),
                   jax.ShapeDtypeStruct((width, width), weight_type), jax.ShapeDtypeStruct((1, width), F32)],
        scratch_shapes=[pltpu.VMEM((rows, width), LOW), pltpu.VMEM((width, rows), LOW)]
        + [pltpu.VMEM((rows, QUAD), LOW)] * 4 + [pltpu.VMEM((rows, width), F32)],
        compiler_params=params(),
        cost_estimate=cost,
    )(grad, x, gain, n, q, k, v, probs, att, qkv, qkv, qkv, out_weight, *extra)


FF_TILE = 512


def run_mlp(second, cot, keep, gain, w1, w2, old=None, weight_type=F32):
    rows, width = second.shape
    hidden = w1.shape[1]
    steps = hidden // FF_TILE
    cost = pl.CostEstimate(flops=12 * rows * width * hidden, bytes_accessed=rows * width * 14 + 12 * width * hidden, transcendentals=rows * hidden)
    weight_out = [spec_cols((width, FF_TILE)), spec_rows((FF_TILE, width)), fixed((1, width))]
    extra = [] if old is None else list(old)
    return pl.pallas_call(
        functools.partial(mlp_both, old is not None),
        grid=(steps,),
        in_specs=[whole((rows, width)), whole((rows, width)), whole((rows, 1)), whole((1, width)),
                  spec_cols((width, FF_TILE)), spec_rows((FF_TILE, width))] + (weight_out if extra else []),
        out_specs=[fixed((rows, width)), fixed((rows, width))] + weight_out,
        out_shape=[jax.ShapeDtypeStruct((rows, width), LOW), jax.ShapeDtypeStruct((rows, width), F32),
                   jax.ShapeDtypeStruct((width, hidden), weight_type), jax.ShapeDtypeStruct((hidden, width), weight_type),
                   jax.ShapeDtypeStruct((1, width), F32)],
        scratch_shapes=[pltpu.VMEM((rows, width), LOW), pltpu.VMEM((width, rows), LOW), pltpu.VMEM((rows, width), LOW),
                        pltpu.VMEM((rows, width), F32), pltpu.VMEM((rows, width), F32),
                        pltpu.VMEM((rows, FF_TILE), LOW), pltpu.VMEM((rows, FF_TILE), LOW)],
        compiler_params=params(),
        cost_estimate=cost,
    )(second, cot, keep, gain, w1, w2, *extra)


GROUP = 8


def to_blocks(v):
    frames, places, width = v.shape
    groups = -(-places // GROUP)
    v = jnp.pad(v, ((0, 0), (0, groups * GROUP - places), (0, 0)))
    return v.reshape(frames, groups, GROUP, width).transpose(1, 0, 2, 3).reshape(groups * frames * GROUP, width)


def from_blocks(v, frames, places):
    width = v.shape[-1]
    v = v.reshape(-1, frames, GROUP, width).transpose(1, 0, 2, 3).reshape(frames, -1, width)
    return v[:, :places]


def to_places(v, parts):
    clips, frames, slots, width = v.shape
    v = v.transpose(1, 0, 2, 3).reshape(frames, parts, clips * slots // parts, width).transpose(1, 0, 2, 3)
    v = lax.all_to_all(v, "seq", split_axis=0, concat_axis=0, tiled=True)
    return v.reshape(parts * frames, clips * slots // parts, width)


def to_frames(v, parts, clips):
    frames, places, width = v.shape
    v = v.reshape(parts, frames // parts, places, width)
    v = lax.all_to_all(v, "seq", split_axis=0, concat_axis=0, tiled=True)
    return v.transpose(1, 0, 2, 3).reshape(frames // parts, clips, parts * places // clips, width).transpose(1, 0, 2, 3)


def shards(parts, frames_in, qkv_spatial, out_spatial, qkv_temporal, out_temporal, mlp_in, mlp_out, gains, place_mask, cotangent):
    both = ("dp", "seq")
    micros, clips, local_frames, slots, width = frames_in.shape
    frames = local_frames * parts
    places = clips * slots // parts
    here = clips * local_frames * slots

    def gather(w):
        return lax.all_gather(w, both, axis=0, tiled=True)

    space_qkv, space_out = gather(qkv_spatial), gather(out_spatial)
    gain_rows = gather(gains).astype(F32).T
    time_qkv, time_out = gather(qkv_temporal), gather(out_temporal)
    grow, shrink = gather(mlp_in), gather(mlp_out)
    gain_space, gain_time, gain_mlp = gain_rows[0:1], gain_rows[1:2], gain_rows[2:3]

    bias_space = jnp.where(place_mask > 0, 0.0, -1000000000.0).astype(F32)[None, :]
    tile_time = frames * GROUP
    spot = jnp.arange(tile_time) % GROUP
    bias_time = jnp.where(spot[:, None] == spot[None, :], 0.0, -1000000000.0).astype(F32)
    bias_time = jnp.concatenate([bias_time, bias_time], axis=0)
    keep = jnp.tile(place_mask.astype(F32), clips)
    keep = lax.dynamic_slice_in_dim(keep, lax.axis_index("seq") * places, places)
    keep = to_blocks(jnp.broadcast_to(keep[None, :, None], (frames, places, 1)))

    spatial, temporal = [], []
    cots = [to_blocks(to_places(cotangent[m], parts)) for m in range(micros)]
    for m in range(micros):
        x = frames_in[m].reshape(here, width)
        out, *saved = run_attend_fwd(x, gain_space, bias_space, space_qkv, space_out, slots, LOW)
        across = to_blocks(to_places(out.reshape(clips, local_frames, slots, width), parts))
        spatial.append((x, saved, across))
    outputs, afters = [], []
    old_mlp = old_time = None
    for m in range(micros):
        last = LOW if m == micros - 1 else F32
        across = spatial[m][2]
        second, *saved = run_attend_fwd(across, gain_time, bias_time, time_qkv, time_out, tile_time, F32)
        out, grad, *old_mlp = run_mlp(second, cots[m], keep, gain_mlp, grow, shrink, old_mlp, last)
        outputs.append(to_frames(from_blocks(out, frames, places), parts, clips))
        after, *old_time = run_attend_bwd(grad, across, gain_time, saved, time_qkv, time_out, tile_time, LOW, old_time, last)
        afters.append(to_frames(from_blocks(after, frames, places), parts, clips))
    input_grads = []
    old_space = None
    for m in range(micros):
        last = LOW if m == micros - 1 else F32
        x, saved, _ = spatial[m]
        grad, *old_space = run_attend_bwd(afters[m].reshape(here, width), x, gain_space, saved, space_qkv, space_out, slots, F32, old_space, last)
        input_grads.append(grad.reshape(clips, local_frames, slots, width))

    def scatter(w, axis=0):
        return lax.psum_scatter(w, both, scatter_dimension=axis, tiled=True)

    def scatter_qkv(w):
        return scatter(w, 1).transpose(1, 0, 2).reshape(-1, 3 * width).astype(F32)

    gain_sum = lax.psum_scatter(jnp.concatenate([old_space[2], old_time[2], old_mlp[2]], axis=0).T, both, scatter_dimension=0, tiled=True)
    return (
        jnp.stack(outputs),
        jnp.stack(input_grads),
        scatter_qkv(old_space[0]),
        scatter(old_space[1]).astype(F32),
        scatter_qkv(old_time[0]),
        scatter(old_time[1]).astype(F32),
        scatter(old_mlp[0]).astype(F32),
        scatter(old_mlp[1]).astype(F32),
        gain_sum,
    )


def solution(mesh):
    rows = P(("dp", "seq"), None)
    tokens = P(None, "dp", "seq", None, None)
    return jax.shard_map(
        functools.partial(shards, mesh.shape["seq"]),
        mesh=mesh,
        in_specs=(tokens,) + (rows,) * 7 + (P(), tokens),
        out_specs=(tokens, tokens) + (rows,) * 7,
        check_vma=False,
    )
```

```python
import functools

import jax
import jax.numpy as jnp
from jax import lax
from jax.experimental import pallas as pl
from jax.experimental.pallas import tpu as pltpu
from jax.sharding import PartitionSpec as P

HEAD_DIM = 64
PAIR = 2 * HEAD_DIM
QUAD = 4 * HEAD_DIM
EPSILON = 1e-06
LOW = jnp.bfloat16
F32 = jnp.float32
VMEM_LIMIT = 60 * 1024 * 1024
COST_SHARE = 10
GELU_A = 0.7978845608028654
GELU_B = 0.044715


def dot(a, b):
    return lax.dot_general(a, b, (((1,), (0,)), ((), ())), preferred_element_type=F32)


def dot_nt(a, b):
    return lax.dot_general(a, b, (((1,), (1,)), ((), ())), preferred_element_type=F32)


def dot_tn(a, b):
    return lax.dot_general(a, b, (((0,), (0,)), ((), ())), preferred_element_type=F32)


def row_block(rows, most=512):
    for parts in range(1, rows + 1):
        if rows % parts == 0 and rows // parts <= most and (rows // parts) % 16 == 0:
            return rows // parts
    return rows


def loop_rows(total, size, body):
    @pl.loop(0, total // size)
    def _(step):
        body(pl.ds(pl.multiple_of(step * size, size), size))


def normalise(v):
    centered = v - jnp.mean(v, axis=-1, keepdims=True)
    spread = jnp.mean(centered * centered, axis=-1, keepdims=True)
    inverse = lax.rsqrt(spread + EPSILON)
    return centered * inverse, inverse


def norm_back(v, gain, grad):
    n, inverse = normalise(v)
    scaled = grad * gain
    back = scaled - jnp.mean(scaled, axis=-1, keepdims=True) - n * jnp.mean(scaled * n, axis=-1, keepdims=True)
    return back * inverse, jnp.sum(grad * n, axis=0, keepdims=True)


def gain_row(gains_ref, column):
    return gains_ref[...].astype(F32).T[column:column + 1]


def half_masks(kind):
    lane = lax.broadcasted_iota(jnp.int32, (1, PAIR), 1)
    first = (lane < HEAD_DIM).astype(F32)
    return first.astype(kind), (1.0 - first).astype(kind)


def spread_pair(v):
    first, second = half_masks(v.dtype)
    return jnp.concatenate([v * first, v * second], axis=0)


def join_pair(v):
    tile = v.shape[0] // 2
    first, second = half_masks(v.dtype)
    return v[:tile] * first + v[tile:] * second


def store_pieces(me, pieces, source_ref, plan):
    for at, piece_ref in enumerate(pieces):
        starts = plan.starts(lax.bitwise_xor(me, at))

        @pl.loop(0, plan.groups)
        def _(group):
            for low in range(0, plan.frames, plan.joint):
                rows = [source_ref[pl.ds(pl.multiple_of(starts[low + more] + group * plan.group, plan.group), plan.group), :] for more in range(plan.joint)]
                piece_ref[group, pl.ds(low * plan.group, 16), :] = jnp.concatenate(rows, axis=0).astype(piece_ref.dtype)


def load_pieces(me, pieces, target_ref, plan):
    for at, piece_ref in enumerate(pieces):
        starts = plan.starts(lax.bitwise_xor(me, at))

        @pl.loop(0, plan.groups)
        def _(group):
            for low in range(0, plan.frames, plan.joint):
                rows = piece_ref[group, pl.ds(low * plan.group, 16), :].astype(F32)
                for more in range(plan.joint):
                    target_ref[pl.ds(pl.multiple_of(starts[low + more] + group * plan.group, plan.group), plan.group), :] = rows[more * plan.group:(more + 1) * plan.group]


class Plan:
    def __init__(self, parts, clips, frames, slots):
        self.parts, self.clips, self.frames = parts, clips, frames
        self.joint = 2 if frames % 2 == 0 else 1
        self.group = 16 // self.joint
        self.per_clip = parts // clips
        self.places = slots // self.per_clip
        self.groups = -(-self.places // self.group)
        self.room = self.groups * self.group
        self.slots = self.room * self.per_clip
        self.span = frames * self.group
        self.tile_time = parts * self.span
        self.rows = clips * frames * self.slots

    def starts(self, part):
        clip, place = part // self.per_clip, part % self.per_clip
        return [(clip * self.frames + frame) * self.slots + place * self.room for frame in range(self.frames)]

    def fill(self, v):
        v = v.reshape(v.shape[:2] + (self.per_clip, self.places) + v.shape[3:])
        return jnp.pad(v, [(0, 0)] * 3 + [(0, self.room - self.places)] + [(0, 0)] * (v.ndim - 4))

    def fill_all(self, v):
        return self.fill(v.reshape((-1,) + v.shape[2:]))

    def strip(self, v, lead):
        v = v.reshape(lead + (self.frames, self.per_clip, self.room, v.shape[-1]))
        return v[..., :self.places, :].reshape(lead + (self.frames, self.per_clip * self.places, v.shape[-1]))


def attend_fwd(plan, space, *refs):
    if space:
        tile = plan.slots
        me_ref, x_ref = refs[0], refs[1].at[0]
        refs = refs[2:]
    else:
        tile = plan.tile_time
        pieces, refs = refs[:plan.parts], refs[plan.parts:]
    gains_ref, bias_ref, wq_ref, wk_ref, wv_ref, wo_ref = refs[:6]
    refs = refs[6:]
    if space:
        out_pieces, refs = refs[:plan.parts], refs[plan.parts:]
    else:
        out_ref, refs = refs[0], refs[1:]
    nt_ref, q_ref, k_ref, v_ref, p_ref, att_ref, n_ref, acc_ref, gain_ref = refs
    step, steps = pl.program_id(0), pl.num_programs(0)
    rows = n_ref.shape[0]
    rb = row_block(rows)
    small = row_block(rows, 64)

    @pl.when(step == 0)
    def _():
        gain_ref[...] = gain_row(gains_ref, 0 if space else 1)

        def take(at, x):
            x = x.astype(F32)
            n_ref[at, :] = (normalise(x)[0] * gain_ref[...]).astype(LOW)
            acc_ref[at, :] = x

        if space:
            loop_rows(rows, small, lambda at: take(at, x_ref[at, :]))
        else:
            @pl.loop(0, plan.groups)
            def _(group):
                for k, piece_ref in enumerate(pieces):
                    take(pl.ds(pl.multiple_of(group * tile + k * plan.span, 16), plan.span), piece_ref[group])
        nt_ref[...] = n_ref[...].T

    def project(at):
        n = n_ref[at, :]
        q_ref[at, :] = (dot(n, wq_ref[...]).astype(LOW) * (HEAD_DIM ** -0.5)).astype(LOW)
        k_ref[at, :] = dot(n, wk_ref[...]).astype(LOW)
        v_ref[at, :] = dot(n, wv_ref[...]).astype(LOW)
    loop_rows(rows, rb, project)

    @pl.loop(0, rows // tile)
    def _(t):
        at = pl.ds(pl.multiple_of(t * tile, tile), tile)
        for pair in range(2):
            cols = pl.ds(pair * PAIR, PAIR)
            qs = spread_pair(q_ref[at, cols])
            s = dot_nt(qs, k_ref[at, cols]) + bias_ref[...]
            e = jnp.exp(s - jnp.max(s, axis=-1, keepdims=True))
            p = (e * (1.0 / jnp.sum(e, axis=-1, keepdims=True))).astype(LOW)
            p_ref[0, pl.ds(pl.multiple_of((t * 2 + pair) * 2 * tile, 2 * tile), 2 * tile), :] = p
            att_ref[at, cols] = join_pair(dot(p, v_ref[at, cols])).astype(LOW)

    def project_out(at):
        acc_ref[at, :] += dot(att_ref[at, :], wo_ref[...])
    loop_rows(rows, rb, project_out)

    @pl.when(step == steps - 1)
    def _():
        if space:
            store_pieces(me_ref[0], out_pieces, acc_ref, plan)
        else:
            out_ref[...] = acc_ref[...]


def attend_bwd(plan, space, prior, again, *refs):
    parts = plan.parts
    if space:
        tile = plan.slots
        me_ref, g_pieces, done_pieces, x_ref, refs = refs[0], refs[1:1 + parts], refs[1 + parts:1 + 2 * parts], refs[1 + 2 * parts].at[0], refs[2 + 2 * parts:]
    else:
        tile = plan.tile_time
        g_ref, x_pieces, refs = refs[0], refs[1:1 + parts], refs[1 + parts:]
    gains_ref, nt_ref, q_ref, k_ref, v_ref, p_ref, att_ref, wq_ref, wk_ref, wv_ref, wo_ref = refs[:11]
    refs = refs[11:]
    if prior:
        old_ref, oldo_ref, oldg_ref = refs[:3]
        refs = refs[3:]
    if again:
        refs = refs[2:]
    if space:
        gx_ref, done_ref, refs = refs[0].at[0], refs[1].at[0], refs[2:]
    else:
        out_pieces, refs = refs[:parts], refs[parts:]
    dw_ref, dwo_ref, dgain_ref, low_ref, do_ref, dq_ref, dk_ref, dv_ref, acc_ref, gain_ref = refs
    step, steps = pl.program_id(0), pl.num_programs(0)
    rows, width = acc_ref.shape
    rb = row_block(rows)
    small = row_block(rows, 64)

    @pl.when(step == 0)
    def _():
        gain_ref[...] = gain_row(gains_ref, 0 if space else 1)
        if space:
            load_pieces(me_ref[0], g_pieces, gx_ref, plan)

            def lower(at):
                low_ref[at, :] = gx_ref[at, :].astype(LOW)
        else:
            def lower(at):
                low_ref[at, :] = g_ref[at, :].astype(LOW)
        loop_rows(rows, small, lower)

    def back_out(at):
        do_ref[at, :] = dot_nt(low_ref[at, :], wo_ref[...]).astype(LOW)
    loop_rows(rows, rb, back_out)
    total = dot_tn(att_ref[...], low_ref[...])
    if prior:
        total += oldo_ref[...]
    dwo_ref[...] = total.astype(dwo_ref.dtype)

    @pl.loop(0, rows // tile)
    def _(t):
        at = pl.ds(pl.multiple_of(t * tile, tile), tile)
        for pair in range(2):
            cols = pl.ds(pair * PAIR, PAIR)
            dos = spread_pair(do_ref[at, cols])
            att = att_ref[at, cols].astype(F32)
            inner = jnp.sum(dos.astype(F32) * jnp.concatenate([att, att], axis=0), axis=-1, keepdims=True)
            p = p_ref[0, pl.ds(pl.multiple_of((t * 2 + pair) * 2 * tile, 2 * tile), 2 * tile), :]
            ds = (p.astype(F32) * (dot_nt(dos, v_ref[at, cols]) - inner)).astype(LOW)
            dq_ref[at, cols] = (join_pair(dot(ds, k_ref[at, cols])) * (HEAD_DIM ** -0.5)).astype(LOW)
            dk_ref[at, cols] = dot_tn(ds, spread_pair(q_ref[at, cols])).astype(LOW)
            dv_ref[at, cols] = dot_tn(p, dos).astype(LOW)

    def back_in(at):
        part = dot_nt(dq_ref[at, :], wq_ref[...]) + dot_nt(dk_ref[at, :], wk_ref[...]) + dot_nt(dv_ref[at, :], wv_ref[...])

        @pl.when(step == 0)
        def _():
            acc_ref[at, :] = part

        @pl.when(step != 0)
        def _():
            acc_ref[at, :] += part
    loop_rows(rows, rb, back_in)
    for at, grad_ref in enumerate((dq_ref, dk_ref, dv_ref)):
        total = dot(nt_ref[...], grad_ref[...])
        if prior:
            total += old_ref[at]
        dw_ref[at] = total.astype(dw_ref.dtype)

    @pl.when(step == steps - 1)
    def _():
        if prior:
            dgain_ref[...] = oldg_ref[...]
        else:
            dgain_ref[...] = jnp.zeros_like(dgain_ref)

        if space:
            def finish(at):
                back, gains = norm_back(x_ref[at, :].astype(F32), gain_ref[...], acc_ref[at, :])
                dgain_ref[...] += gains
                gx_ref[at, :] += back
            loop_rows(rows, small, finish)
            load_pieces(me_ref[0], done_pieces, acc_ref, plan)

            def lower(at):
                done_ref[at, :] = acc_ref[at, :].astype(LOW)
            loop_rows(rows, small, lower)
        else:
            @pl.loop(0, plan.groups)
            def _(group):
                for k in range(parts):
                    at = pl.ds(pl.multiple_of(group * tile + k * plan.span, 16), plan.span)
                    back, gains = norm_back(x_pieces[k][group].astype(F32), gain_ref[...], acc_ref[at, :])
                    dgain_ref[...] += gains
                    out_pieces[k][group] = (g_ref[at, :] + back).astype(LOW)


def mlp_both(plan, prior, me_ref, second_ref, cot_ref, *refs):
    parts = plan.parts
    keep_ref, gains_ref, w1_ref, w2_ref = refs[:4]
    refs = refs[4:]
    if prior:
        old1_ref, old2_ref, oldg_ref = refs[:3]
        refs = refs[3:]
    out_pieces, refs = refs[:parts], refs[parts:]
    grad_ref, dw1_ref, dw2_ref, dgain_ref, n_ref, nt_ref, up_ref, sum_ref, act_ref, gh_ref, gain_ref = refs
    acc_ref = grad_ref
    step, steps = pl.program_id(0), pl.num_programs(0)
    rows = second_ref.shape[0]
    rb = row_block(rows, 256)

    def each_span(body):
        @pl.loop(0, plan.groups)
        def _(group):
            for k in range(parts):
                body(group, k, pl.ds(pl.multiple_of(group * plan.tile_time + k * plan.span, 16), plan.span))

    @pl.when(step == 0)
    def _():
        gain_ref[...] = gain_row(gains_ref, 2)

        def start(group, k, at):
            v = second_ref[at, :]
            n_ref[at, :] = (normalise(v)[0] * gain_ref[...]).astype(LOW)
            up_ref[at, :] = (cot_ref[lax.bitwise_xor(me_ref[0], k), group].astype(F32) * keep_ref[at, :]).astype(LOW)
            sum_ref[at, :] = v
            acc_ref[at, :] = jnp.zeros_like(v)
        each_span(start)
        nt_ref[...] = n_ref[...].T

    width = second_ref.shape[1]
    firsts = [pl.ds(at * UNITS, UNITS) for at in range(FF_TILE // UNITS)]
    seconds = [pl.ds(at * width, width) for at in range(FF_TILE // UNITS)]

    def body(at):
        h = dot(n_ref[at, :], w1_ref[...])
        ga = jnp.concatenate([dot_nt(up_ref[at, :], w2_ref[:, second]) for second in seconds], axis=1)
        square = h * h
        t = jnp.tanh(GELU_A * h * (1.0 + GELU_B * square))
        half = 0.5 + 0.5 * t
        act = (h * half).astype(LOW)
        slope = half + h * (0.5 - 0.5 * t * t) * (GELU_A + (3.0 * GELU_A * GELU_B) * square)
        gh = (ga * slope).astype(LOW)
        act_ref[at, :] = act
        gh_ref[at, :] = gh
        sum_ref[at, :] += sum(dot(act[:, first.start:first.start + first.size], w2_ref[:, second]) for first, second in zip(firsts, seconds))
        acc_ref[at, :] += dot_nt(gh, w1_ref[...])
    loop_rows(rows, rb, body)
    total = dot(nt_ref[...], gh_ref[...])
    if prior:
        total += old1_ref[...]
    dw1_ref[...] = total.astype(dw1_ref.dtype)
    for first, second in zip(firsts, seconds):
        total = dot_tn(act_ref[:, first], up_ref[...])
        if prior:
            total += old2_ref[:, second]
        dw2_ref[:, second] = total.astype(dw2_ref.dtype)

    @pl.when(step == steps - 1)
    def _():
        if prior:
            dgain_ref[...] = oldg_ref[...]
        else:
            dgain_ref[...] = jnp.zeros_like(dgain_ref)

        def last(group, k, at):
            out_pieces[k][group] = (keep_ref[at, :] * sum_ref[at, :]).astype(LOW)
            back, gains = norm_back(second_ref[at, :], gain_ref[...], acc_ref[at, :])
            dgain_ref[...] += gains
            grad_ref[at, :] = up_ref[at, :].astype(F32) + back
        each_span(last)


def whole(shape, at=None):
    spot = (0,) * len(shape) if at is None else at
    return pl.BlockSpec(shape, lambda i: spot, pipeline_mode=pl.Buffered(1))


def params():
    return pltpu.CompilerParams(dimension_semantics=("arbitrary",), vmem_limit_bytes=VMEM_LIMIT)


def spec_cols(shape, offset=0):
    return pl.BlockSpec(shape, lambda i, o=offset: (0, o + i))


def spec_rows(shape, column=0):
    return pl.BlockSpec(shape, lambda i: (i, column))


def weight_specs(width):
    quads = width // QUAD
    return [spec_cols((width, QUAD), at * quads) for at in range(3)] + [spec_rows((QUAD, width), 3)]


def piece_shapes(plan, width):
    return [jax.ShapeDtypeStruct((plan.groups, plan.span, width), LOW)] * plan.parts


def piece_specs(plan, width):
    return [whole((plan.groups, plan.span, width))] * plan.parts


def scalar():
    return pl.BlockSpec(memory_space=pltpu.SMEM)


LANES = 128


def gains_spec(bundle):
    rows, columns = bundle.shape
    return whole((rows, LANES), (0, columns // LANES - 1))


def run_attend_fwd(plan, space, micro, lead, gain, bias, weights):
    rows, width = plan.rows, gain.shape[0]
    tile = plan.slots if space else plan.tile_time
    quads = width // QUAD
    probs_rows = rows * 4
    low = jax.ShapeDtypeStruct((rows, width), LOW)
    cost = pl.CostEstimate(flops=rows * 4 // COST_SHARE * width * (4 * width + 8 * tile), bytes_accessed=rows * width, transcendentals=0)
    lead_specs = [scalar(), whole((1, rows, width), (micro, 0, 0))] if space else piece_specs(plan, width)
    out_specs = piece_specs(plan, width) if space else [whole((rows, width))]
    out_shape = piece_shapes(plan, width) if space else [jax.ShapeDtypeStruct((rows, width), F32)]
    result = pl.pallas_call(
        functools.partial(attend_fwd, plan, space),
        grid=(quads,),
        in_specs=lead_specs + [gains_spec(gain), whole(bias.shape)] + weight_specs(width),
        out_specs=out_specs + [whole((width, rows))] + [spec_cols((rows, QUAD))] * 3
        + [pl.BlockSpec((1, probs_rows, tile), lambda i: (i, 0, 0)), spec_cols((rows, QUAD))],
        out_shape=out_shape + [jax.ShapeDtypeStruct((width, rows), LOW), low, low, low,
                               jax.ShapeDtypeStruct((quads, probs_rows, tile), LOW), low],
        scratch_shapes=[pltpu.VMEM((rows, width), LOW), pltpu.VMEM((rows, width), F32), pltpu.VMEM((1, width), F32)],
        compiler_params=params(),
        cost_estimate=cost,
    )(*lead, gain, bias, weights, weights, weights, weights)
    return list(result[:len(out_shape)]), list(result[len(out_shape):])


def run_attend_bwd(plan, space, lead, gain, saved, weights, micro, micros, old=None, shared=None):
    rows, width = plan.rows, gain.shape[0]
    tile = plan.slots if space else plan.tile_time
    quads = width // QUAD
    probs_rows = rows * 4
    weight_type = LOW if micro == micros - 1 else F32
    cost = pl.CostEstimate(flops=rows * 4 // COST_SHARE * width * (8 * width + 20 * tile), bytes_accessed=rows * width, transcendentals=0)
    weight_out = [pl.BlockSpec((3, width, QUAD), lambda i: (0, 0, i)), spec_rows((QUAD, width)), whole((1, width))]
    token = whole((rows, width))
    lead_specs = [scalar()] + piece_specs(plan, width) * 2 + [whole((1, rows, width), (micro, 0, 0))] if space else [token] + piece_specs(plan, width)
    if space:
        out_specs = [whole((1, rows, width), (micro, 0, 0))] * 2
        out_shape = [jax.ShapeDtypeStruct((micros, rows, width), F32), jax.ShapeDtypeStruct((micros, rows, width), LOW)]
    else:
        out_specs, out_shape = piece_specs(plan, width), piece_shapes(plan, width)
    operands = [*lead, gain, *saved, weights, weights, weights, weights]
    in_specs = (lead_specs + [gains_spec(gain), whole((width, rows))] + [spec_cols((rows, QUAD))] * 3
                + [pl.BlockSpec((1, probs_rows, tile), lambda i: (i, 0, 0)), spec_cols((rows, QUAD))] + weight_specs(width))
    if old is not None:
        operands += old
        in_specs = in_specs + weight_out
    aliases = {}
    if shared is not None:
        aliases = {len(operands): 0, len(operands) + 1: 1}
        operands += shared
        in_specs = in_specs + [pl.BlockSpec(memory_space=pl.ANY)] * 2
    result = pl.pallas_call(
        functools.partial(attend_bwd, plan, space, old is not None, shared is not None),
        grid=(quads,),
        in_specs=in_specs,
        out_specs=out_specs + weight_out,
        out_shape=out_shape + [jax.ShapeDtypeStruct((3, width, width), weight_type),
                               jax.ShapeDtypeStruct((width, width), weight_type), jax.ShapeDtypeStruct((1, width), F32)],
        scratch_shapes=[pltpu.VMEM((rows, width), LOW)] + [pltpu.VMEM((rows, QUAD), LOW)] * 4 + [pltpu.VMEM((rows, width), F32), pltpu.VMEM((1, width), F32)],
        input_output_aliases=aliases,
        compiler_params=params(),
        cost_estimate=cost,
    )(*operands)
    return list(result[:len(out_shape)]), list(result[len(out_shape):])


FF_TILE = 512
UNITS = 256


def run_mlp(plan, me, second, cot, keep, gain, weights, last, old=None):
    rows, width = second.shape
    hidden = weights.shape[1] // 2
    steps = hidden // FF_TILE
    joint = FF_TILE // UNITS
    blocks = width // UNITS
    weight_type = LOW if last else F32
    cost = pl.CostEstimate(flops=rows * 14 // COST_SHARE * width * hidden, bytes_accessed=rows * width, transcendentals=0)

    def second_spec(start):
        return pl.BlockSpec((UNITS, joint * width), lambda i: (i % blocks, start // (joint * width) + i // blocks))
    weight_out = [spec_cols((width, FF_TILE)), second_spec(0), whole((1, width))]
    token = whole((rows, width))
    result = pl.pallas_call(
        functools.partial(mlp_both, plan, old is not None),
        grid=(steps,),
        in_specs=[scalar(), token, whole(cot.shape), whole((rows, 1)), gains_spec(gain),
                  spec_cols((width, FF_TILE)), second_spec(hidden)] + ([] if old is None else weight_out),
        out_specs=piece_specs(plan, width) + [token] + weight_out,
        out_shape=piece_shapes(plan, width) + [jax.ShapeDtypeStruct((rows, width), F32),
                   jax.ShapeDtypeStruct((width, hidden), weight_type), jax.ShapeDtypeStruct((width, hidden), weight_type),
                   jax.ShapeDtypeStruct((1, width), F32)],
        scratch_shapes=[pltpu.VMEM((rows, width), LOW), pltpu.VMEM((width, rows), LOW), pltpu.VMEM((rows, width), LOW),
                        pltpu.VMEM((rows, width), F32),
                        pltpu.VMEM((rows, FF_TILE), LOW), pltpu.VMEM((rows, FF_TILE), LOW), pltpu.VMEM((1, width), F32)],
        compiler_params=params(),
        cost_estimate=cost,
    )(me, second, cot, keep, gain, weights, weights, *([] if old is None else old))
    return list(result[:plan.parts]), result[plan.parts], list(result[plan.parts + 1:])


class Units:
    def __init__(self, devices, width, hidden):
        self.devices, self.rows = devices, width // devices
        self.ratio, self.joint = hidden // width, FF_TILE // UNITS
        self.blocks = width // UNITS

    def first_in(self, v):
        lead = v.shape[0]
        v = v.reshape(lead, self.devices, self.ratio, self.rows).transpose(0, 2, 1, 3)
        v = v.reshape(lead, self.ratio // self.joint, self.joint, self.blocks, UNITS).transpose(0, 1, 3, 2, 4)
        return v.reshape(lead, -1)

    def first_out(self, v):
        lead = v.shape[0]
        v = v.reshape(lead, self.ratio // self.joint, self.blocks, self.joint, UNITS).transpose(0, 1, 3, 2, 4)
        v = v.reshape(lead, self.ratio, self.devices, self.rows).transpose(0, 2, 1, 3)
        return v.reshape(lead, -1)

    def second_in(self, v):
        return v.reshape(self.ratio, self.rows, -1).transpose(1, 0, 2).reshape(self.rows, -1)

    def second_out(self, v):
        return v.reshape(self.rows, self.ratio, -1).transpose(1, 0, 2).reshape(self.rows * self.ratio, -1)


def swap(v, axis, size, by):
    return lax.ppermute(v, axis, [(i, i ^ by) for i in range(size)])


def exchange(pieces):
    return [piece if at == 0 else swap(piece, "seq", len(pieces), at) for at, piece in enumerate(pieces)]


def pick(v, at):
    return lax.dynamic_index_in_dim(v, at, 0, False)


def collect(v, axis, size, me, stride=1):
    count = size * stride
    out = jnp.zeros((size,) + v.shape, v.dtype)
    for at in range(size):
        out = lax.dynamic_update_index_in_dim(out, v if at == 0 else swap(v, axis, count, at * stride), lax.bitwise_xor(me, at), 0)
    return out


def reduce_blocks(v, axis, size, me, stride=1):
    count = size * stride
    parts = [swap(pick(v, lax.bitwise_xor(me, at)), axis, count, at * stride) for at in range(1, size)]
    total = pick(v, me).astype(F32)
    for part in parts:
        total += part.astype(F32)
    return total


def gather_rows(v, dp, seq):
    rows, width = v.shape
    device, place = lax.axis_index("dp"), lax.axis_index("seq")
    v = collect(v, "seq", seq, place)
    v = collect(v, "dp", dp // 2, device // 2, 2)
    other = swap(v, "dp", dp, 1)
    core = (device % 2) == 0
    v = jnp.stack([jnp.where(core, v, other), jnp.where(core, other, v)], axis=1)
    return v.reshape(dp * seq * rows, width)


def scatter_rows(v, dp, seq):
    device, place = lax.axis_index("dp"), lax.axis_index("seq")
    rows, width = v.shape
    v = v.reshape(dp // 2, 2, rows // dp, width)
    core = device % 2
    own = lax.dynamic_index_in_dim(v, core, 1, False)
    got = swap(lax.dynamic_index_in_dim(v, 1 - core, 1, False), "dp", dp, 1)
    v = (own.astype(F32) + got.astype(F32)).astype(LOW)
    v = reduce_blocks(v, "dp", dp // 2, device // 2, 2).astype(LOW)
    return reduce_blocks(v.reshape(seq, rows // (dp * seq), width), "seq", seq, place)


def shards(dp, seq, frames_in, qkv_spatial, out_spatial, qkv_temporal, out_temporal, mlp_in, mlp_out, gains, place_mask, cotangent):
    both = ("dp", "seq")
    micros, clips, local_frames, slots, width = frames_in.shape
    hidden = mlp_in.shape[1]
    plan = Plan(seq, clips, local_frames, slots)
    place = lax.axis_index("seq")
    me = place.astype(jnp.int32).reshape(1)

    units = Units(dp * seq, width, hidden)
    after = lax.optimization_barrier

    def send_cot(v):
        v = plan.fill(v).transpose(0, 2, 1, 3, 4).reshape(seq, local_frames, plan.groups, plan.group, width)
        v = v.transpose(0, 2, 1, 3, 4).reshape(seq, plan.groups, plan.span, width)
        return lax.all_to_all(v, "seq", split_axis=0, concat_axis=0, tiled=True)

    padded_gains = jnp.pad(gains, ((0, 0), (0, LANES - gains.shape[1])))
    cots = [send_cot(cotangent[0])]
    space = gather_rows(jnp.concatenate([qkv_spatial, out_spatial, padded_gains], axis=1), dp, seq)
    time = lax.all_gather(jnp.concatenate([qkv_temporal, out_temporal], axis=1), both, axis=0, tiled=True)
    mlp = lax.all_gather(jnp.concatenate([units.first_in(mlp_in), units.second_in(mlp_out)], axis=1), both, axis=0, tiled=True)

    bias_space = jnp.where(place_mask > 0, 0.0, -1000000000.0).astype(F32).reshape(plan.per_clip, plan.places)
    bias_space = jnp.pad(bias_space, ((0, 0), (0, plan.room - plan.places)), constant_values=-1000000000.0).reshape(1, plan.slots)
    spot = jnp.arange(plan.tile_time) % plan.group
    bias_time = jnp.where(spot[:, None] == spot[None, :], 0.0, -1000000000.0).astype(F32)
    bias_time = jnp.concatenate([bias_time, bias_time], axis=0)
    keep = pick(place_mask.astype(F32).reshape(plan.per_clip, plan.places), place % plan.per_clip)
    keep = jnp.pad(keep, (0, plan.room - plan.places)).reshape(plan.groups, 1, plan.group)
    keep = jnp.broadcast_to(keep, (plan.groups, seq * local_frames, plan.group)).reshape(plan.rows, 1)

    inputs = plan.fill_all(frames_in).reshape(micros, plan.rows, width)
    space_saved, across = [], []
    for m in range(micros):
        out, saved = run_attend_fwd(plan, True, m, [me, inputs], space, bias_space, space)
        space_saved.append(saved)
        across.append(exchange(out))
        if m == 0:
            me, cots[0] = after((me, cots[0]))
    def scatter(parts):
        return lax.psum_scatter(jnp.concatenate(parts, axis=1), both, scatter_dimension=0, tiled=True).astype(F32)

    def attend_parts(old):
        return [old[0][0], old[0][1], old[0][2], old[1]]

    done, afters, time_saved, grads = [], [], [], []
    old_mlp = old_time = old_space = shared = None
    for m in range(micros):
        (second,), saved = run_attend_fwd(plan, False, m, across[m], space, bias_time, time)
        time_saved.append(saved)
        if m > 0:
            second, done[m - 1] = after((second, done[m - 1]))
        if m + 1 < micros:
            second, across, cot = after((second, across, cotangent[m + 1]))
            cots.append(send_cot(cot))
            across[m + 1], cots[m + 1] = after((across[m + 1], cots[m + 1]))
        out, grad, old_mlp = run_mlp(plan, me, second, cots[m], keep, space, mlp, m == micros - 1, old_mlp)
        done.append(exchange(out))
        grads.append(grad)
    owned_mlp = scatter(old_mlp[:2])
    for m in range(micros):
        grads[m], old_mlp[2] = after((grads[m], old_mlp[2]))
        if m > 0:
            grads[m], done[-1] = after((grads[m], done[-1]))
        back, old_time = run_attend_bwd(plan, False, [grads[m], *across[m]], space, time_saved[m], time, m, micros, old_time)
        afters.append(exchange(back))
    owned_time = scatter(attend_parts(old_time))
    afters[0], old_time[2] = after((afters[0], old_time[2]))
    for m in range(micros):
        if m == micros - 1:
            afters[m], owned_mlp = after((afters[m], owned_mlp))
        shared, old_space = run_attend_bwd(plan, True, [me, *afters[m], *done[m], inputs], space, space_saved[m], space, m, micros, old_space, shared)

    gain_grads = jnp.concatenate([old_space[2], old_time[2], old_mlp[2]], axis=0).T.astype(LOW)
    owned = scatter_rows(jnp.concatenate(attend_parts(old_space) + [jnp.pad(gain_grads, ((0, 0), (0, LANES - gain_grads.shape[1])))], axis=1), dp, seq)
    return (
        plan.strip(shared[1], (micros, clips)),
        plan.strip(shared[0], (micros, clips)),
        owned[:, :3 * width],
        owned[:, 3 * width:4 * width],
        owned_time[:, :3 * width],
        owned_time[:, 3 * width:],
        units.first_out(owned_mlp[:, :hidden]),
        units.second_out(owned_mlp[:, hidden:]),
        owned[:, 4 * width:4 * width + gains.shape[1]],
    )


def solution(mesh):
    rows = P(("dp", "seq"), None)
    tokens = P(None, "dp", "seq", None, None)
    return jax.shard_map(
        functools.partial(shards, mesh.shape["dp"], mesh.shape["seq"]),
        mesh=mesh,
        in_specs=(tokens,) + (rows,) * 7 + (P(), tokens),
        out_specs=(tokens, tokens) + (rows,) * 7,
        check_vma=False,
    )
```

```python
import functools

import jax
import jax.numpy as jnp
from jax import lax
from jax.experimental import pallas as pl
from jax.experimental.pallas import tpu as pltpu
from jax.sharding import PartitionSpec as P

HEAD_DIM = 64
PAIR = 2 * HEAD_DIM
QUAD = 4 * HEAD_DIM
EPSILON = 1e-06
LOW = jnp.bfloat16
F32 = jnp.float32
VMEM_LIMIT = 62 * 1024 * 1024
COST_SHARE = 10
EARLY = 3
GELU_A = 0.7978845608028654
GELU_B = 0.044715


def dot(a, b):
    return lax.dot_general(a, b, (((1,), (0,)), ((), ())), preferred_element_type=F32)


def dot_nt(a, b):
    return lax.dot_general(a, b, (((1,), (1,)), ((), ())), preferred_element_type=F32)


def dot_tn(a, b):
    return lax.dot_general(a, b, (((0,), (0,)), ((), ())), preferred_element_type=F32)


def row_block(rows, most=512):
    for parts in range(1, rows + 1):
        if rows % parts == 0 and rows // parts <= most and (rows // parts) % 16 == 0:
            return rows // parts
    return rows


def loop_rows(total, size, body):
    @pl.loop(0, total // size)
    def _(step):
        body(pl.ds(pl.multiple_of(step * size, size), size))


def loop_tiles(tiles, tile, joint, body):
    def spots(first, count):
        found = []
        for t in range(count):
            for pair in range(2):
                start = pl.multiple_of((first + t) * tile, tile)
                kept = pl.multiple_of(((first + t) * 2 + pair) * 2 * tile, 2 * tile)
                found.append((pl.ds(start, tile), pl.ds(pair * PAIR, PAIR), pl.ds(kept, 2 * tile)))
        return found

    joint = min(joint, tiles)

    @pl.loop(0, tiles // joint)
    def _(step):
        body(spots(step * joint, joint))
    if tiles % joint:
        body(spots(tiles - tiles % joint, tiles % joint))


TILES_FWD_SPACE, TILES_FWD_TIME, TILES_BWD_SPACE, TILES_BWD_TIME = 8, 13, 8, 13
SMALL, UNROLL_PIECES, UNROLL_SPANS = 208, 16, 2


def normalise(v):
    centered = v - jnp.mean(v, axis=-1, keepdims=True)
    spread = jnp.mean(centered * centered, axis=-1, keepdims=True)
    inverse = lax.rsqrt(spread + EPSILON)
    return centered * inverse, inverse


def norm_back(v, gain, grad):
    n, inverse = normalise(v)
    scaled = grad * gain
    back = scaled - jnp.mean(scaled, axis=-1, keepdims=True) - n * jnp.mean(scaled * n, axis=-1, keepdims=True)
    return back * inverse, jnp.sum(grad * n, axis=0, keepdims=True)


def gain_row(gains_ref, column):
    return gains_ref[...].astype(F32).T[column:column + 1]


def half_masks(kind):
    lane = lax.broadcasted_iota(jnp.int32, (1, PAIR), 1)
    first = (lane < HEAD_DIM).astype(F32)
    return first.astype(kind), (1.0 - first).astype(kind)


def spread_pair(v):
    first, second = half_masks(v.dtype)
    return jnp.concatenate([v * first, v * second], axis=0)


def join_pair(v):
    tile = v.shape[0] // 2
    first, second = half_masks(v.dtype)
    return v[:tile] * first + v[tile:] * second


def store_pieces(me, pieces, source_ref, plan):
    for at, piece_ref in enumerate(pieces):
        starts = plan.starts(lax.bitwise_xor(me, at))

        @pl.loop(0, plan.groups, unroll=min(UNROLL_PIECES, plan.groups))
        def _(group):
            for low in range(0, plan.frames, plan.joint):
                rows = [source_ref[pl.ds(pl.multiple_of(starts[low + more] + group * plan.group, plan.group), plan.group), :] for more in range(plan.joint)]
                piece_ref[group, pl.ds(low * plan.group, 16), :] = jnp.concatenate(rows, axis=0).astype(piece_ref.dtype)


def load_pieces(me, pieces, target_ref, plan):
    for at, piece_ref in enumerate(pieces):
        starts = plan.starts(lax.bitwise_xor(me, at))

        @pl.loop(0, plan.groups, unroll=min(UNROLL_PIECES, plan.groups))
        def _(group):
            for low in range(0, plan.frames, plan.joint):
                rows = piece_ref[group, pl.ds(low * plan.group, 16), :].astype(F32)
                for more in range(plan.joint):
                    target_ref[pl.ds(pl.multiple_of(starts[low + more] + group * plan.group, plan.group), plan.group), :] = rows[more * plan.group:(more + 1) * plan.group]


class Plan:
    def __init__(self, parts, clips, frames, slots):
        self.parts, self.clips, self.frames = parts, clips, frames
        self.joint = 2 if frames % 2 == 0 else 1
        self.group = 16 // self.joint
        self.per_clip = parts // clips
        self.places = slots // self.per_clip
        self.groups = -(-self.places // self.group)
        self.room = self.groups * self.group
        self.slots = self.room * self.per_clip
        self.span = frames * self.group
        self.tile_time = parts * self.span
        self.rows = clips * frames * self.slots

    def starts(self, part):
        clip, place = part // self.per_clip, part % self.per_clip
        return [(clip * self.frames + frame) * self.slots + place * self.room for frame in range(self.frames)]

    def fill(self, v):
        v = v.reshape(v.shape[:2] + (self.per_clip, self.places) + v.shape[3:])
        return jnp.pad(v, [(0, 0)] * 3 + [(0, self.room - self.places)] + [(0, 0)] * (v.ndim - 4))

    def fill_all(self, v):
        return self.fill(v.reshape((-1,) + v.shape[2:]))

    def strip(self, v, lead):
        v = v.reshape(lead + (self.frames, self.per_clip, self.room, v.shape[-1]))
        return v[..., :self.places, :].reshape(lead + (self.frames, self.per_clip * self.places, v.shape[-1]))


def attend_fwd(plan, space, *refs):
    if space:
        tile = plan.slots
        me_ref, x_ref = refs[0], refs[1].at[0]
        refs = refs[2:]
    else:
        tile = plan.tile_time
        pieces, refs = refs[:plan.parts], refs[plan.parts:]
    gains_ref, bias_ref, wq_ref, wk_ref, wv_ref, wo_ref = refs[:6]
    refs = refs[6:]
    if space:
        out_pieces, refs = refs[:plan.parts], refs[plan.parts:]
    else:
        out_ref, refs = refs[0], refs[1:]
    nt_ref, q_ref, k_ref, v_ref, p_ref, att_ref, n_ref, acc_ref, gain_ref = refs
    step, steps = pl.program_id(0), pl.num_programs(0)
    rows = n_ref.shape[0]
    rb = row_block(rows)
    small = row_block(rows, SMALL)

    @pl.when(step == 0)
    def _():
        gain_ref[...] = gain_row(gains_ref, 0 if space else 1)

        def take(at, x):
            x = x.astype(F32)
            n_ref[at, :] = (normalise(x)[0] * gain_ref[...]).astype(LOW)
            acc_ref[at, :] = x

        if space:
            loop_rows(rows, small, lambda at: take(at, x_ref[at, :]))
        else:
            @pl.loop(0, plan.groups, unroll=min(UNROLL_SPANS, plan.groups))
            def _(group):
                for k, piece_ref in enumerate(pieces):
                    take(pl.ds(pl.multiple_of(group * tile + k * plan.span, 16), plan.span), piece_ref[group])
        nt_ref[...] = n_ref[...].T

    def project(at):
        n = n_ref[at, :]
        q_ref[at, :] = (dot(n, wq_ref[...]).astype(LOW) * (HEAD_DIM ** -0.5)).astype(LOW)
        k_ref[at, :] = dot(n, wk_ref[...]).astype(LOW)
        v_ref[at, :] = dot(n, wv_ref[...]).astype(LOW)
    loop_rows(rows, rb, project)

    def attend(spots):
        scores = [dot_nt(spread_pair(q_ref[at, cols]), k_ref[at, cols]) + bias_ref[...] for at, cols, _ in spots]
        scores = [jnp.exp(score - jnp.max(score, axis=-1, keepdims=True)) for score in scores]
        scores = [(score * (1.0 / jnp.sum(score, axis=-1, keepdims=True))).astype(LOW) for score in scores]
        results = [dot(score, v_ref[at, cols]) for score, (at, cols, _) in zip(scores, spots)]
        for score, result, (at, cols, kept) in zip(scores, results, spots):
            p_ref[0, kept, :] = score
            att_ref[at, cols] = join_pair(result).astype(LOW)
    loop_tiles(rows // tile, tile, TILES_FWD_SPACE if space else TILES_FWD_TIME, attend)

    def project_out(at):
        acc_ref[at, :] += dot(att_ref[at, :], wo_ref[...])
    loop_rows(rows, rb, project_out)

    @pl.when(step == steps - 1)
    def _():
        if space:
            store_pieces(me_ref[0], out_pieces, acc_ref, plan)
        else:
            out_ref[...] = acc_ref[...]


def attend_bwd(plan, space, prior, again, deliver, *refs):
    parts = plan.parts
    if space:
        tile = plan.slots
        me_ref, g_pieces, x_ref, refs = refs[0], refs[1:1 + parts], refs[1 + parts].at[0], refs[2 + parts:]
        if deliver:
            done_pieces, refs = refs[:parts], refs[parts:]
    else:
        tile = plan.tile_time
        g_ref, x_pieces, refs = refs[0], refs[1:1 + parts], refs[1 + parts:]
    gains_ref, nt_ref, q_ref, k_ref, v_ref, p_ref, att_ref, wq_ref, wk_ref, wv_ref, wo_ref = refs[:11]
    refs = refs[11:]
    if prior:
        old_ref, oldo_ref, oldg_ref = refs[:3]
        refs = refs[3:]
    if again:
        refs = refs[1:]
    if space:
        gx_ref, refs = refs[0].at[0], refs[1:]
        if deliver:
            done_ref, refs = refs[0].at[0], refs[1:]
    else:
        out_pieces, refs = refs[:parts], refs[parts:]
    dw_ref, dwo_ref, dgain_ref, low_ref, do_ref, dq_ref, dk_ref, dv_ref, acc_ref, gain_ref = refs
    step, steps = pl.program_id(0), pl.num_programs(0)
    rows, width = acc_ref.shape
    rb = row_block(rows)
    small = row_block(rows, SMALL)

    @pl.when(step == 0)
    def _():
        gain_ref[...] = gain_row(gains_ref, 0 if space else 1)
        if space:
            load_pieces(me_ref[0], g_pieces, gx_ref, plan)

            def lower(at):
                low_ref[at, :] = gx_ref[at, :].astype(LOW)
        else:
            def lower(at):
                low_ref[at, :] = g_ref[at, :].astype(LOW)
        loop_rows(rows, small, lower)

    def back_out(at):
        do_ref[at, :] = dot_nt(low_ref[at, :], wo_ref[...]).astype(LOW)
    loop_rows(rows, rb, back_out)
    total = dot_tn(att_ref[...], low_ref[...])
    if prior:
        total += oldo_ref[...]
    dwo_ref[...] = total.astype(dwo_ref.dtype)

    def attend(spots):
        outs = [spread_pair(do_ref[at, cols]) for at, cols, _ in spots]
        atts = [att_ref[at, cols].astype(F32) for at, cols, _ in spots]
        inners = [jnp.sum(out.astype(F32) * jnp.concatenate([att, att], axis=0), axis=-1, keepdims=True) for out, att in zip(outs, atts)]
        probs = [p_ref[0, kept, :] for _, _, kept in spots]
        values = [dot_tn(prob, out).astype(LOW) for prob, out in zip(probs, outs)]
        scores = [dot_nt(out, v_ref[at, cols]) for out, (at, cols, _) in zip(outs, spots)]
        scores = [(prob.astype(F32) * (score - inner)).astype(LOW) for prob, score, inner in zip(probs, scores, inners)]
        queries = [(join_pair(dot(score, k_ref[at, cols])) * (HEAD_DIM ** -0.5)).astype(LOW) for score, (at, cols, _) in zip(scores, spots)]
        keys = [dot_tn(score, spread_pair(q_ref[at, cols])).astype(LOW) for score, (at, cols, _) in zip(scores, spots)]
        for query, key, value, (at, cols, _) in zip(queries, keys, values, spots):
            dq_ref[at, cols] = query
            dk_ref[at, cols] = key
            dv_ref[at, cols] = value
    loop_tiles(rows // tile, tile, TILES_BWD_SPACE if space else TILES_BWD_TIME, attend)

    def back_in(at):
        part = dot_nt(dq_ref[at, :], wq_ref[...]) + dot_nt(dk_ref[at, :], wk_ref[...]) + dot_nt(dv_ref[at, :], wv_ref[...])

        @pl.when(step == 0)
        def _():
            acc_ref[at, :] = part

        @pl.when(step != 0)
        def _():
            acc_ref[at, :] += part
    loop_rows(rows, rb, back_in)
    for at, grad_ref in enumerate((dq_ref, dk_ref, dv_ref)):
        total = dot(nt_ref[...], grad_ref[...])
        if prior:
            total += old_ref[at]
        dw_ref[at] = total.astype(dw_ref.dtype)

    @pl.when(step == steps - 1)
    def _():
        if prior:
            dgain_ref[...] = oldg_ref[...]
        else:
            dgain_ref[...] = jnp.zeros_like(dgain_ref)

        if space:
            def finish(at):
                back, gains = norm_back(x_ref[at, :].astype(F32), gain_ref[...], acc_ref[at, :])
                dgain_ref[...] += gains
                gx_ref[at, :] += back
            loop_rows(rows, small, finish)
            if deliver:
                load_pieces(me_ref[0], done_pieces, acc_ref, plan)

                def lower(at):
                    done_ref[at, :] = acc_ref[at, :].astype(LOW)
                loop_rows(rows, small, lower)
        else:
            @pl.loop(0, plan.groups, unroll=min(UNROLL_SPANS, plan.groups))
            def _(group):
                for k in range(parts):
                    at = pl.ds(pl.multiple_of(group * tile + k * plan.span, 16), plan.span)
                    back, gains = norm_back(x_pieces[k][group].astype(F32), gain_ref[...], acc_ref[at, :])
                    dgain_ref[...] += gains
                    out_pieces[k][group] = (g_ref[at, :] + back).astype(LOW)


def mlp_both(plan, prior, second_ref, *refs):
    parts = plan.parts
    cot_pieces, refs = refs[:parts], refs[parts:]
    keep_ref, gains_ref, w1_ref, w2_ref = refs[:4]
    refs = refs[4:]
    if prior:
        old1_ref, old2_ref, oldg_ref = refs[:3]
        refs = refs[3:]
    out_pieces, refs = refs[:parts], refs[parts:]
    grad_ref, dw1_ref, dw2_ref, dgain_ref, n_ref, nt_ref, up_ref, sum_ref, act_ref, gh_ref, gain_ref = refs
    acc_ref = grad_ref
    step, steps = pl.program_id(0), pl.num_programs(0)
    rows = second_ref.shape[0]
    rb = row_block(rows)

    def each_span(body):
        @pl.loop(0, plan.groups, unroll=min(UNROLL_SPANS, plan.groups))
        def _(group):
            for k in range(parts):
                body(group, k, pl.ds(pl.multiple_of(group * plan.tile_time + k * plan.span, 16), plan.span))

    @pl.when(step == 0)
    def _():
        gain_ref[...] = gain_row(gains_ref, 2)

        def start(group, k, at):
            v = second_ref[at, :]
            n_ref[at, :] = (normalise(v)[0] * gain_ref[...]).astype(LOW)
            up_ref[at, :] = (cot_pieces[k][group].astype(F32) * keep_ref[at, :]).astype(LOW)
            sum_ref[at, :] = v
            acc_ref[at, :] = jnp.zeros_like(v)
        each_span(start)
        nt_ref[...] = n_ref[...].T

    width = second_ref.shape[1]
    firsts = [pl.ds(at * UNITS, UNITS) for at in range(FF_TILE // UNITS)]
    seconds = [pl.ds(at * width, width) for at in range(FF_TILE // UNITS)]

    def body(at):
        h = dot(n_ref[at, :], w1_ref[...])
        ga = jnp.concatenate([dot_nt(up_ref[at, :], w2_ref[:, second]) for second in seconds], axis=1)
        square = h * h
        t = jnp.tanh(GELU_A * h * (1.0 + GELU_B * square))
        half = 0.5 + 0.5 * t
        act = (h * half).astype(LOW)
        slope = half + h * (0.5 - 0.5 * t * t) * (GELU_A + (3.0 * GELU_A * GELU_B) * square)
        gh = (ga * slope).astype(LOW)
        act_ref[at, :] = act
        gh_ref[at, :] = gh
        sum_ref[at, :] += sum(dot(act[:, first.start:first.start + first.size], w2_ref[:, second]) for first, second in zip(firsts, seconds))
        acc_ref[at, :] += dot_nt(gh, w1_ref[...])
    loop_rows(rows, rb, body)
    total = dot(nt_ref[...], gh_ref[...])
    if prior:
        total += old1_ref[...]
    dw1_ref[...] = total.astype(dw1_ref.dtype)
    for first, second in zip(firsts, seconds):
        total = dot_tn(act_ref[:, first], up_ref[...])
        if prior:
            total += old2_ref[:, second]
        dw2_ref[:, second] = total.astype(dw2_ref.dtype)

    @pl.when(step == steps - 1)
    def _():
        if prior:
            dgain_ref[...] = oldg_ref[...]
        else:
            dgain_ref[...] = jnp.zeros_like(dgain_ref)

        def last(group, k, at):
            out_pieces[k][group] = (keep_ref[at, :] * sum_ref[at, :]).astype(LOW)
            back, gains = norm_back(second_ref[at, :], gain_ref[...], acc_ref[at, :])
            dgain_ref[...] += gains
            grad_ref[at, :] = up_ref[at, :].astype(F32) + back
        each_span(last)


def whole(shape, at=None):
    spot = (0,) * len(shape) if at is None else at
    return pl.BlockSpec(shape, lambda i: spot, pipeline_mode=pl.Buffered(1))


def params():
    return pltpu.CompilerParams(dimension_semantics=("arbitrary",), vmem_limit_bytes=VMEM_LIMIT)


def spec_cols(shape, offset=0):
    return pl.BlockSpec(shape, lambda i, o=offset: (0, o + i))


def spec_rows(shape, column=0):
    return pl.BlockSpec(shape, lambda i: (i, column))


def weight_specs(width):
    quads = width // QUAD
    return [spec_cols((width, QUAD), at * quads) for at in range(3)] + [spec_rows((QUAD, width), 3)]


def piece_shapes(plan, width):
    return [jax.ShapeDtypeStruct((plan.groups, plan.span, width), LOW)] * plan.parts


def piece_specs(plan, width):
    return [whole((plan.groups, plan.span, width))] * plan.parts


def scalar():
    return pl.BlockSpec(memory_space=pltpu.SMEM)


LANES = 128


def gains_spec(bundle):
    rows, columns = bundle.shape
    return whole((rows, LANES), (0, columns // LANES - 1))


def run_attend_fwd(plan, space, micro, lead, gain, bias, weights):
    rows, width = plan.rows, gain.shape[0]
    tile = plan.slots if space else plan.tile_time
    quads = width // QUAD
    probs_rows = rows * 4
    low = jax.ShapeDtypeStruct((rows, width), LOW)
    cost = pl.CostEstimate(flops=rows * 4 // COST_SHARE * width * (4 * width + 8 * tile), bytes_accessed=rows * width, transcendentals=0)
    lead_specs = [scalar(), whole((1, rows, width), (micro, 0, 0))] if space else piece_specs(plan, width)
    out_specs = piece_specs(plan, width) if space else [whole((rows, width))]
    out_shape = piece_shapes(plan, width) if space else [jax.ShapeDtypeStruct((rows, width), F32)]
    result = pl.pallas_call(
        functools.partial(attend_fwd, plan, space),
        grid=(quads,),
        in_specs=lead_specs + [gains_spec(gain), whole(bias.shape)] + weight_specs(width),
        out_specs=out_specs + [whole((width, rows))] + [spec_cols((rows, QUAD))] * 3
        + [pl.BlockSpec((1, probs_rows, tile), lambda i: (i, 0, 0)), spec_cols((rows, QUAD))],
        out_shape=out_shape + [jax.ShapeDtypeStruct((width, rows), LOW), low, low, low,
                               jax.ShapeDtypeStruct((quads, probs_rows, tile), LOW), low],
        scratch_shapes=[pltpu.VMEM((rows, width), LOW), pltpu.VMEM((rows, width), F32), pltpu.VMEM((1, width), F32)],
        compiler_params=params(),
        cost_estimate=cost,
    )(*lead, gain, bias, weights, weights, weights, weights)
    return list(result[:len(out_shape)]), list(result[len(out_shape):])


def run_attend_bwd(plan, space, lead, gain, saved, weights, micro, micros, old=None, shared=None):
    rows, width = plan.rows, gain.shape[0]
    tile = plan.slots if space else plan.tile_time
    quads = width // QUAD
    probs_rows = rows * 4
    weight_type = LOW if micro == micros - 1 else F32
    cost = pl.CostEstimate(flops=rows * 4 // COST_SHARE * width * (8 * width + 20 * tile), bytes_accessed=rows * width, transcendentals=0)
    weight_out = [pl.BlockSpec((3, width, QUAD), lambda i: (0, 0, i)), spec_rows((QUAD, width)), whole((1, width))]
    token = whole((rows, width))
    deliver = space and micro + 1 < micros
    lead_specs = [scalar()] + piece_specs(plan, width) + [whole((1, rows, width), (micro, 0, 0))] + (piece_specs(plan, width) if deliver else []) if space else [token] + piece_specs(plan, width)
    if space:
        out_specs = [whole((1, rows, width), (micro, 0, 0))] * (1 + deliver)
        out_shape = [jax.ShapeDtypeStruct((micros, rows, width), kind) for kind in ((F32, LOW) if deliver else (F32,))]
    else:
        out_specs, out_shape = piece_specs(plan, width), piece_shapes(plan, width)
    operands = [*lead, gain, *saved, weights, weights, weights, weights]
    in_specs = (lead_specs + [gains_spec(gain), whole((width, rows))] + [spec_cols((rows, QUAD))] * 3
                + [pl.BlockSpec((1, probs_rows, tile), lambda i: (i, 0, 0)), spec_cols((rows, QUAD))] + weight_specs(width))
    if old is not None:
        operands += old
        in_specs = in_specs + weight_out
    aliases = {}
    if shared is not None:
        aliases = {len(operands): 0}
        operands += shared[:1]
        in_specs = in_specs + [pl.BlockSpec(memory_space=pl.ANY)]
    result = pl.pallas_call(
        functools.partial(attend_bwd, plan, space, old is not None, shared is not None, deliver),
        grid=(quads,),
        in_specs=in_specs,
        out_specs=out_specs + weight_out,
        out_shape=out_shape + [jax.ShapeDtypeStruct((3, width, width), weight_type),
                               jax.ShapeDtypeStruct((width, width), weight_type), jax.ShapeDtypeStruct((1, width), F32)],
        scratch_shapes=[pltpu.VMEM((rows, width), LOW)] + [pltpu.VMEM((rows, QUAD), LOW)] * 4 + [pltpu.VMEM((rows, width), F32), pltpu.VMEM((1, width), F32)],
        input_output_aliases=aliases,
        compiler_params=params(),
        cost_estimate=cost,
    )(*operands)
    return list(result[:len(out_shape)]), list(result[len(out_shape):])


FF_TILE = 512
UNITS = 256


def run_mlp(plan, second, cots, keep, gain, weights, last, old=None):
    rows, width = second.shape
    hidden = weights.shape[1] // 2
    steps = hidden // FF_TILE
    joint = FF_TILE // UNITS
    blocks = width // UNITS
    weight_type = LOW if last else F32
    cost = pl.CostEstimate(flops=rows * 14 // COST_SHARE * width * hidden, bytes_accessed=rows * width, transcendentals=0)

    def second_spec(start):
        return pl.BlockSpec((UNITS, joint * width), lambda i: (i % blocks, start // (joint * width) + i // blocks))
    weight_out = [spec_cols((width, FF_TILE)), second_spec(0), whole((1, width))]
    token = whole((rows, width))
    result = pl.pallas_call(
        functools.partial(mlp_both, plan, old is not None),
        grid=(steps,),
        in_specs=[token] + piece_specs(plan, width) + [whole((rows, 1)), gains_spec(gain),
                  spec_cols((width, FF_TILE)), second_spec(hidden)] + ([] if old is None else weight_out),
        out_specs=piece_specs(plan, width) + [token] + weight_out,
        out_shape=piece_shapes(plan, width) + [jax.ShapeDtypeStruct((rows, width), F32),
                   jax.ShapeDtypeStruct((width, hidden), weight_type), jax.ShapeDtypeStruct((width, hidden), weight_type),
                   jax.ShapeDtypeStruct((1, width), F32)],
        scratch_shapes=[pltpu.VMEM((rows, width), LOW), pltpu.VMEM((width, rows), LOW), pltpu.VMEM((rows, width), LOW),
                        pltpu.VMEM((rows, width), F32),
                        pltpu.VMEM((rows, FF_TILE), LOW), pltpu.VMEM((rows, FF_TILE), LOW), pltpu.VMEM((1, width), F32)],
        compiler_params=params(),
        cost_estimate=cost,
    )(second, *cots, keep, gain, weights, weights, *([] if old is None else old))
    return list(result[:plan.parts]), result[plan.parts], list(result[plan.parts + 1:])


class Units:
    def __init__(self, devices, width, hidden):
        self.devices, self.rows = devices, width // devices
        self.ratio, self.joint = hidden // width, FF_TILE // UNITS
        self.blocks = width // UNITS

    def first_in(self, v):
        lead = v.shape[0]
        v = v.reshape(lead, self.devices, self.ratio, self.rows).transpose(0, 2, 1, 3)
        v = v.reshape(lead, self.ratio // self.joint, self.joint, self.blocks, UNITS).transpose(0, 1, 3, 2, 4)
        return v.reshape(lead, -1)

    def first_out(self, v):
        lead = v.shape[0]
        v = v.reshape(lead, self.ratio // self.joint, self.blocks, self.joint, UNITS).transpose(0, 1, 3, 2, 4)
        v = v.reshape(lead, self.ratio, self.devices, self.rows).transpose(0, 2, 1, 3)
        return v.reshape(lead, -1)

    def second_in(self, v):
        return v.reshape(self.ratio, self.rows, -1).transpose(1, 0, 2).reshape(self.rows, -1)

    def second_out(self, v):
        return v.reshape(self.rows, self.ratio, -1).transpose(1, 0, 2).reshape(self.rows * self.ratio, -1)


def swap(v, axis, size, by):
    return lax.ppermute(v, axis, [(i, i ^ by) for i in range(size)])


def exchange(pieces):
    return [piece if at == 0 else swap(piece, "seq", len(pieces), at) for at, piece in enumerate(pieces)]


def pick(v, at):
    return lax.dynamic_index_in_dim(v, at, 0, False)


def collect(v, axis, size, me, stride=1):
    count = size * stride
    out = jnp.zeros((size,) + v.shape, v.dtype)
    for at in range(size):
        out = lax.dynamic_update_index_in_dim(out, v if at == 0 else swap(v, axis, count, at * stride), lax.bitwise_xor(me, at), 0)
    return out


def reduce_blocks(v, axis, size, me, stride=1):
    count = size * stride
    parts = [swap(pick(v, lax.bitwise_xor(me, at)), axis, count, at * stride) for at in range(1, size)]
    total = pick(v, me).astype(F32)
    for part in parts:
        total += part.astype(F32)
    return total


def join_cores(v, dp):
    other = swap(v, "dp", dp, 1)
    core = (lax.axis_index("dp") % 2) == 0
    v = jnp.stack([jnp.where(core, v, other), jnp.where(core, other, v)], axis=1)
    return v.reshape(-1, v.shape[-1])


def scatter_rows(v, dp, seq):
    device, place = lax.axis_index("dp"), lax.axis_index("seq")
    rows, width = v.shape
    v = v.reshape(dp // 2, 2, rows // dp, width)
    core = device % 2
    own = lax.dynamic_index_in_dim(v, core, 1, False)
    got = swap(lax.dynamic_index_in_dim(v, 1 - core, 1, False), "dp", dp, 1)
    v = (own.astype(F32) + got.astype(F32)).astype(LOW)
    v = reduce_blocks(v, "dp", dp // 2, device // 2, 2).astype(LOW)
    return reduce_blocks(v.reshape(seq, rows // (dp * seq), width), "seq", seq, place)


def shards(dp, seq, frames_in, qkv_spatial, out_spatial, qkv_temporal, out_temporal, mlp_in, mlp_out, gains, place_mask, cotangent):
    micros, clips, local_frames, slots, width = frames_in.shape
    hidden = mlp_in.shape[1]
    plan = Plan(seq, clips, local_frames, slots)
    place = lax.axis_index("seq")
    me = place.astype(jnp.int32).reshape(1)

    units = Units(dp * seq, width, hidden)
    after = lax.optimization_barrier

    def cot_pieces(v):
        v = plan.fill(v).transpose(0, 2, 1, 3, 4).reshape(seq, local_frames, plan.groups, plan.group, width)
        return [pick(v, lax.bitwise_xor(place, at)).transpose(1, 0, 2, 3).reshape(plan.groups, plan.span, width) for at in range(seq)]

    padded_gains = jnp.pad(gains, ((0, 0), (0, LANES - gains.shape[1])))
    space = jnp.concatenate([qkv_spatial, out_spatial, padded_gains], axis=1)
    rest = lax.all_gather(jnp.concatenate([qkv_temporal, out_temporal, units.first_in(mlp_in), units.second_in(mlp_out)], axis=1), "seq", axis=0, tiled=True)
    cots = [exchange(cot_pieces(cotangent[0]))]
    space = collect(space, "seq", seq, place)
    device = lax.axis_index("dp")
    space = collect(space, "dp", dp // 2, device // 2, 2)
    space, cots[0][:EARLY] = after((space, cots[0][:EARLY]))
    space = join_cores(space, dp)
    bias_space = jnp.where(place_mask > 0, 0.0, -1000000000.0).astype(F32).reshape(plan.per_clip, plan.places)
    bias_space = jnp.pad(bias_space, ((0, 0), (0, plan.room - plan.places)), constant_values=-1000000000.0).reshape(1, plan.slots)
    spot = jnp.arange(plan.tile_time) % plan.group
    bias_time = jnp.where(spot[:, None] == spot[None, :], 0.0, -1000000000.0).astype(F32)
    bias_time = jnp.concatenate([bias_time, bias_time], axis=0)
    keep = pick(place_mask.astype(F32).reshape(plan.per_clip, plan.places), place % plan.per_clip)
    keep = jnp.pad(keep, (0, plan.room - plan.places)).reshape(plan.groups, 1, plan.group)
    keep = jnp.broadcast_to(keep, (plan.groups, seq * local_frames, plan.group)).reshape(plan.rows, 1)

    inputs = plan.fill_all(frames_in).reshape(micros, plan.rows, width)
    space_saved, across = [], []
    for m in range(micros):
        out, saved = run_attend_fwd(plan, True, m, [me, inputs], space, bias_space, space)
        space_saved.append(saved)
        across.append(exchange(out))
        if m == 0:
            rest, _ = after((rest, out[0]))
            time = lax.all_gather(rest[:, :4 * width], "dp", axis=0, tiled=True)
            mlp = lax.all_gather(rest[:, 4 * width:], "dp", axis=0, tiled=True)
            me, cots[0] = after((me, cots[0]))

    def scatter(parts):
        v = lax.psum_scatter(jnp.concatenate(parts, axis=1), "dp", scatter_dimension=0, tiled=True)
        return reduce_blocks(v.reshape(seq, v.shape[0] // seq, -1), "seq", seq, place)

    def attend_parts(old):
        return [old[0][0], old[0][1], old[0][2], old[1]]

    done, afters, time_saved, grads = [], [], [], []
    old_mlp = old_time = old_space = shared = None
    outs = []
    for m in range(micros):
        (second,), saved = run_attend_fwd(plan, False, m, across[m], space, bias_time, time)
        time_saved.append(saved)
        if m > 0:
            second, outs[m - 1] = after((second, outs[m - 1]))
            done.append(exchange(outs[m - 1]))
        if m + 1 < micros:
            second, across[m + 1], cot = after((second, across[m + 1], cotangent[m + 1]))
            cots.append(exchange(cot_pieces(cot)))
        out, grad, old_mlp = run_mlp(plan, second, cots[m], keep, space, mlp, m == micros - 1, old_mlp)
        outs.append(out)
        grads.append(grad)
        if m + 1 < micros:
            across[m + 1], cots[m + 1], old_mlp[2] = after((across[m + 1], cots[m + 1], old_mlp[2]))
    old_mlp, done = after((old_mlp, done))
    owned_mlp = scatter(old_mlp[:2])
    for m in range(micros):
        grads[m], old_mlp[2], done = after((grads[m], old_mlp[2], done))
        back, old_time = run_attend_bwd(plan, False, [grads[m], *across[m]], space, time_saved[m], time, m, micros, old_time)
        afters.append(exchange(back))
    old_time, afters[0] = after((old_time, afters[0]))
    owned_time = scatter(attend_parts(old_time))
    for m in range(micros):
        if m == micros - 1:
            afters[m], owned_mlp = after((afters[m], owned_mlp))
        result, old_space = run_attend_bwd(plan, True, [me, *afters[m], inputs] + (done[m] if m + 1 < micros else []), space, space_saved[m], space, m, micros, old_space, shared)
        shared = result + (shared or [])[1:]
        if m + 1 == micros - 1:
            old_space[2], outs[-1] = after((old_space[2], outs[-1]))
            final = exchange(outs[-1])

    old_space, final = after((old_space, final))
    final = jnp.stack(final).reshape(seq, plan.groups, local_frames, plan.group, width).transpose(0, 2, 1, 3, 4)
    for at in range(seq.bit_length() - 1):
        final = final.reshape(seq >> (at + 1), 2, 1 << at, local_frames, plan.room, width)
        final = jnp.where(((place >> at) & 1) == 1, final[:, ::-1], final)
    final = final.reshape(clips, plan.per_clip, local_frames, plan.room, width).transpose(0, 2, 1, 3, 4).reshape(plan.rows, width)
    frames_out = lax.dynamic_update_index_in_dim(shared[1], final, micros - 1, 0)

    gain_grads = jnp.concatenate([old_space[2], old_time[2], old_mlp[2]], axis=0).T.astype(LOW)
    owned = scatter_rows(jnp.concatenate(attend_parts(old_space) + [jnp.pad(gain_grads, ((0, 0), (0, LANES - gain_grads.shape[1])))], axis=1), dp, seq)
    return (
        plan.strip(frames_out, (micros, clips)),
        plan.strip(shared[0], (micros, clips)),
        owned[:, :3 * width],
        owned[:, 3 * width:4 * width],
        owned_time[:, :3 * width],
        owned_time[:, 3 * width:],
        units.first_out(owned_mlp[:, :hidden]),
        units.second_out(owned_mlp[:, hidden:]),
        owned[:, 4 * width:4 * width + gains.shape[1]],
    )


def solution(mesh):
    rows = P(("dp", "seq"), None)
    tokens = P(None, "dp", "seq", None, None)
    return jax.shard_map(
        functools.partial(shards, mesh.shape["dp"], mesh.shape["seq"]),
        mesh=mesh,
        in_specs=(tokens,) + (rows,) * 7 + (P(), tokens),
        out_specs=(tokens, tokens) + (rows,) * 7,
        check_vma=False,
    )
```

```python
import functools

import jax
import jax.numpy as jnp
from jax import lax
from jax.experimental import pallas as pl
from jax.experimental.pallas import tpu as pltpu
from jax.sharding import PartitionSpec as P

HEAD_DIM = 64
PAIR = 2 * HEAD_DIM
QUAD = 4 * HEAD_DIM
EPSILON = 1e-06
LOW = jnp.bfloat16
F32 = jnp.float32
VMEM_LIMIT = 62 * 1024 * 1024
COST_SHARE = 10
EARLY = 3
GELU_A = 0.7978845608028654
GELU_B = 0.044715


def dot(a, b):
    return lax.dot_general(a, b, (((1,), (0,)), ((), ())), preferred_element_type=F32)


def dot_nt(a, b):
    return lax.dot_general(a, b, (((1,), (1,)), ((), ())), preferred_element_type=F32)


def dot_tn(a, b):
    return lax.dot_general(a, b, (((0,), (0,)), ((), ())), preferred_element_type=F32)


def row_block(rows, most=512):
    for parts in range(1, rows + 1):
        if rows % parts == 0 and rows // parts <= most and (rows // parts) % 16 == 0:
            return rows // parts
    return rows


def loop_rows(total, size, body):
    @pl.loop(0, total // size)
    def _(step):
        body(pl.ds(pl.multiple_of(step * size, size), size))


def loop_tiles(tiles, tile, joint, body):
    def spots(first, count):
        found = []
        for t in range(count):
            for pair in range(2):
                start = pl.multiple_of((first + t) * tile, tile)
                kept = pl.multiple_of(((first + t) * 2 + pair) * 2 * tile, 2 * tile)
                found.append((pl.ds(start, tile), pl.ds(pair * PAIR, PAIR), pl.ds(kept, 2 * tile)))
        return found

    joint = min(joint, tiles)

    @pl.loop(0, tiles // joint)
    def _(step):
        body(spots(step * joint, joint))
    if tiles % joint:
        body(spots(tiles - tiles % joint, tiles % joint))


TILES_FWD_SPACE, TILES_FWD_TIME, TILES_BWD_SPACE, TILES_BWD_TIME = 8, 13, 8, 13
SMALL, UNROLL_PIECES, UNROLL_SPANS = 208, 16, 2


def normalise(v):
    centered = v - jnp.mean(v, axis=-1, keepdims=True)
    spread = jnp.mean(centered * centered, axis=-1, keepdims=True)
    inverse = lax.rsqrt(spread + EPSILON)
    return centered * inverse, inverse


def norm_back(v, gain, grad):
    n, inverse = normalise(v)
    scaled = grad * gain
    back = scaled - jnp.mean(scaled, axis=-1, keepdims=True) - n * jnp.mean(scaled * n, axis=-1, keepdims=True)
    return back * inverse, jnp.sum(grad * n, axis=0, keepdims=True)


def gain_row(gains_ref, column):
    return gains_ref[...].astype(F32).T[column:column + 1]


def half_masks(kind):
    lane = lax.broadcasted_iota(jnp.int32, (1, PAIR), 1)
    first = (lane < HEAD_DIM).astype(F32)
    return first.astype(kind), (1.0 - first).astype(kind)


def spread_pair(v):
    first, second = half_masks(v.dtype)
    return jnp.concatenate([v * first, v * second], axis=0)


def join_pair(v):
    tile = v.shape[0] // 2
    first, second = half_masks(v.dtype)
    return v[:tile] * first + v[tile:] * second


def store_pieces(me, pieces, source_ref, plan):
    for at, piece_ref in enumerate(pieces):
        starts = plan.starts(lax.bitwise_xor(me, at))

        @pl.loop(0, plan.groups, unroll=min(UNROLL_PIECES, plan.groups))
        def _(group):
            for low in range(0, plan.frames, plan.joint):
                rows = [source_ref[pl.ds(pl.multiple_of(starts[low + more] + group * plan.group, plan.group), plan.group), :] for more in range(plan.joint)]
                piece_ref[group, pl.ds(low * plan.group, 16), :] = jnp.concatenate(rows, axis=0).astype(piece_ref.dtype)


def load_pieces(me, pieces, target_ref, plan):
    for at, piece_ref in enumerate(pieces):
        starts = plan.starts(lax.bitwise_xor(me, at))

        @pl.loop(0, plan.groups, unroll=min(UNROLL_PIECES, plan.groups))
        def _(group):
            for low in range(0, plan.frames, plan.joint):
                rows = piece_ref[group, pl.ds(low * plan.group, 16), :].astype(F32)
                for more in range(plan.joint):
                    target_ref[pl.ds(pl.multiple_of(starts[low + more] + group * plan.group, plan.group), plan.group), :] = rows[more * plan.group:(more + 1) * plan.group]


class Plan:
    def __init__(self, parts, clips, frames, slots):
        self.parts, self.clips, self.frames = parts, clips, frames
        self.joint = 2 if frames % 2 == 0 else 1
        self.group = 16 // self.joint
        self.per_clip = parts // clips
        self.places = slots // self.per_clip
        self.groups = -(-self.places // self.group)
        self.room = self.groups * self.group
        self.slots = self.room * self.per_clip
        self.span = frames * self.group
        self.tile_time = parts * self.span
        self.rows = clips * frames * self.slots

    def starts(self, part):
        clip, place = part // self.per_clip, part % self.per_clip
        return [(clip * self.frames + frame) * self.slots + place * self.room for frame in range(self.frames)]

    def fill(self, v):
        v = v.reshape(v.shape[:2] + (self.per_clip, self.places) + v.shape[3:])
        return jnp.pad(v, [(0, 0)] * 3 + [(0, self.room - self.places)] + [(0, 0)] * (v.ndim - 4))

    def fill_all(self, v):
        return self.fill(v.reshape((-1,) + v.shape[2:]))

    def strip(self, v, lead):
        v = v.reshape(lead + (self.frames, self.per_clip, self.room, v.shape[-1]))
        return v[..., :self.places, :].reshape(lead + (self.frames, self.per_clip * self.places, v.shape[-1]))


def attend_fwd(plan, space, *refs):
    if space:
        tile = plan.slots
        me_ref, x_ref = refs[0], refs[1].at[0]
        refs = refs[2:]
    else:
        tile = plan.tile_time
        pieces, refs = refs[:plan.parts], refs[plan.parts:]
    gains_ref, bias_ref, wq_ref, wk_ref, wv_ref, wo_ref = refs[:6]
    refs = refs[6:]
    if space:
        out_pieces, refs = refs[:plan.parts], refs[plan.parts:]
    else:
        out_ref, refs = refs[0], refs[1:]
    nt_ref, q_ref, k_ref, v_ref, p_ref, att_ref, n_ref, acc_ref, gain_ref = refs
    step, steps = pl.program_id(0), pl.num_programs(0)
    rows = n_ref.shape[0]
    rb = row_block(rows)
    small = row_block(rows, SMALL)

    @pl.when(step == 0)
    def _():
        gain_ref[...] = gain_row(gains_ref, 0 if space else 1)

        def take(at, x):
            x = x.astype(F32)
            n_ref[at, :] = (normalise(x)[0] * gain_ref[...]).astype(LOW)
            acc_ref[at, :] = x

        if space:
            loop_rows(rows, small, lambda at: take(at, x_ref[at, :]))
        else:
            @pl.loop(0, plan.groups, unroll=min(UNROLL_SPANS, plan.groups))
            def _(group):
                for k, piece_ref in enumerate(pieces):
                    take(pl.ds(pl.multiple_of(group * tile + k * plan.span, 16), plan.span), piece_ref[group])
        nt_ref[...] = n_ref[...].T

    def project(at):
        n = n_ref[at, :]
        q_ref[at, :] = (dot(n, wq_ref[...]).astype(LOW) * (HEAD_DIM ** -0.5)).astype(LOW)
        k_ref[at, :] = dot(n, wk_ref[...]).astype(LOW)
        v_ref[at, :] = dot(n, wv_ref[...]).astype(LOW)
    loop_rows(rows, rb, project)

    def attend(spots):
        scores = [dot_nt(spread_pair(q_ref[at, cols]), k_ref[at, cols]) + bias_ref[...] for at, cols, _ in spots]
        scores = [jnp.exp(score - jnp.max(score, axis=-1, keepdims=True)) for score in scores]
        scores = [(score * (1.0 / jnp.sum(score, axis=-1, keepdims=True))).astype(LOW) for score in scores]
        results = [dot(score, v_ref[at, cols]) for score, (at, cols, _) in zip(scores, spots)]
        for score, result, (at, cols, kept) in zip(scores, results, spots):
            p_ref[0, kept, :] = score
            att_ref[at, cols] = join_pair(result).astype(LOW)
    loop_tiles(rows // tile, tile, TILES_FWD_SPACE if space else TILES_FWD_TIME, attend)

    def project_out(at):
        acc_ref[at, :] += dot(att_ref[at, :], wo_ref[...])
    loop_rows(rows, rb, project_out)

    @pl.when(step == steps - 1)
    def _():
        if space:
            store_pieces(me_ref[0], out_pieces, acc_ref, plan)
        else:
            out_ref[...] = acc_ref[...]


def attend_bwd(plan, space, prior, again, deliver, *refs):
    parts = plan.parts
    if space:
        tile = plan.slots
        me_ref, g_pieces, x_ref, refs = refs[0], refs[1:1 + parts], refs[1 + parts].at[0], refs[2 + parts:]
        if deliver:
            done_pieces, refs = refs[:parts], refs[parts:]
    else:
        tile = plan.tile_time
        g_ref, x_pieces, refs = refs[0], refs[1:1 + parts], refs[1 + parts:]
    gains_ref, nt_ref, q_ref, k_ref, v_ref, p_ref, att_ref, wq_ref, wk_ref, wv_ref, wo_ref = refs[:11]
    refs = refs[11:]
    if prior:
        old_ref, oldo_ref, oldg_ref = refs[:3]
        refs = refs[3:]
    if again:
        refs = refs[2:]
    if space:
        gx_ref, refs = refs[0].at[0], refs[1:]
        if deliver:
            done_ref, refs = refs[0].at[0], refs[1:]
    else:
        out_pieces, refs = refs[:parts], refs[parts:]
    dw_ref, dwo_ref, dgain_ref, low_ref, do_ref, dq_ref, dk_ref, dv_ref, acc_ref, gain_ref = refs
    step, steps = pl.program_id(0), pl.num_programs(0)
    rows, width = acc_ref.shape
    rb = row_block(rows)
    small = row_block(rows, SMALL)

    @pl.when(step == 0)
    def _():
        gain_ref[...] = gain_row(gains_ref, 0 if space else 1)
        if space:
            load_pieces(me_ref[0], g_pieces, gx_ref, plan)

            def lower(at):
                low_ref[at, :] = gx_ref[at, :].astype(LOW)
        else:
            def lower(at):
                low_ref[at, :] = g_ref[at, :].astype(LOW)
        loop_rows(rows, small, lower)

    def back_out(at):
        do_ref[at, :] = dot_nt(low_ref[at, :], wo_ref[...]).astype(LOW)
    loop_rows(rows, rb, back_out)
    total = dot_tn(att_ref[...], low_ref[...])
    if prior:
        total += oldo_ref[...]
    dwo_ref[...] = total.astype(dwo_ref.dtype)

    def attend(spots):
        outs = [spread_pair(do_ref[at, cols]) for at, cols, _ in spots]
        atts = [att_ref[at, cols].astype(F32) for at, cols, _ in spots]
        inners = [jnp.sum(out.astype(F32) * jnp.concatenate([att, att], axis=0), axis=-1, keepdims=True) for out, att in zip(outs, atts)]
        probs = [p_ref[0, kept, :] for _, _, kept in spots]
        values = [dot_tn(prob, out).astype(LOW) for prob, out in zip(probs, outs)]
        scores = [dot_nt(out, v_ref[at, cols]) for out, (at, cols, _) in zip(outs, spots)]
        scores = [(prob.astype(F32) * (score - inner)).astype(LOW) for prob, score, inner in zip(probs, scores, inners)]
        queries = [(join_pair(dot(score, k_ref[at, cols])) * (HEAD_DIM ** -0.5)).astype(LOW) for score, (at, cols, _) in zip(scores, spots)]
        keys = [dot_tn(score, spread_pair(q_ref[at, cols])).astype(LOW) for score, (at, cols, _) in zip(scores, spots)]
        for query, key, value, (at, cols, _) in zip(queries, keys, values, spots):
            dq_ref[at, cols] = query
            dk_ref[at, cols] = key
            dv_ref[at, cols] = value
    loop_tiles(rows // tile, tile, TILES_BWD_SPACE if space else TILES_BWD_TIME, attend)

    def back_in(at):
        part = dot_nt(dq_ref[at, :], wq_ref[...]) + dot_nt(dk_ref[at, :], wk_ref[...]) + dot_nt(dv_ref[at, :], wv_ref[...])

        @pl.when(step == 0)
        def _():
            acc_ref[at, :] = part

        @pl.when(step != 0)
        def _():
            acc_ref[at, :] += part
    loop_rows(rows, rb, back_in)
    for at, grad_ref in enumerate((dq_ref, dk_ref, dv_ref)):
        total = dot(nt_ref[...], grad_ref[...])
        if prior:
            total += old_ref[at]
        dw_ref[at] = total.astype(dw_ref.dtype)

    @pl.when(step == steps - 1)
    def _():
        if prior:
            dgain_ref[...] = oldg_ref[...]
        else:
            dgain_ref[...] = jnp.zeros_like(dgain_ref)

        if space:
            def finish(at):
                back, gains = norm_back(x_ref[at, :].astype(F32), gain_ref[...], acc_ref[at, :])
                dgain_ref[...] += gains
                gx_ref[at, :] += back
            loop_rows(rows, small, finish)
            if deliver:
                load_pieces(me_ref[0], done_pieces, acc_ref, plan)

                def lower(at):
                    done_ref[at, :] = acc_ref[at, :].astype(LOW)
                loop_rows(rows, small, lower)
        else:
            @pl.loop(0, plan.groups, unroll=min(UNROLL_SPANS, plan.groups))
            def _(group):
                for k in range(parts):
                    at = pl.ds(pl.multiple_of(group * tile + k * plan.span, 16), plan.span)
                    back, gains = norm_back(x_pieces[k][group].astype(F32), gain_ref[...], acc_ref[at, :])
                    dgain_ref[...] += gains
                    out_pieces[k][group] = (g_ref[at, :] + back).astype(LOW)


def mlp_both(plan, prior, second_ref, *refs):
    parts = plan.parts
    cot_pieces, refs = refs[:parts], refs[parts:]
    keep_ref, gains_ref, w1_ref, w2_ref = refs[:4]
    refs = refs[4:]
    if prior:
        old1_ref, old2_ref, oldg_ref = refs[:3]
        refs = refs[3:]
    out_pieces, refs = refs[:parts], refs[parts:]
    grad_ref, dw1_ref, dw2_ref, dgain_ref, n_ref, nt_ref, up_ref, sum_ref, act_ref, gh_ref, gain_ref = refs
    acc_ref = grad_ref
    step, steps = pl.program_id(0), pl.num_programs(0)
    rows = second_ref.shape[0]
    rb = row_block(rows)

    def each_span(body):
        @pl.loop(0, plan.groups, unroll=min(UNROLL_SPANS, plan.groups))
        def _(group):
            for k in range(parts):
                body(group, k, pl.ds(pl.multiple_of(group * plan.tile_time + k * plan.span, 16), plan.span))

    @pl.when(step == 0)
    def _():
        gain_ref[...] = gain_row(gains_ref, 2)

        def start(group, k, at):
            v = second_ref[at, :]
            n_ref[at, :] = (normalise(v)[0] * gain_ref[...]).astype(LOW)
            up_ref[at, :] = (cot_pieces[k][group].astype(F32) * keep_ref[at, :]).astype(LOW)
            sum_ref[at, :] = v
            acc_ref[at, :] = jnp.zeros_like(v)
        each_span(start)
        nt_ref[...] = n_ref[...].T

    width = second_ref.shape[1]
    firsts = [pl.ds(at * UNITS, UNITS) for at in range(FF_TILE // UNITS)]
    seconds = [pl.ds(at * width, width) for at in range(FF_TILE // UNITS)]

    def body(at):
        h = dot(n_ref[at, :], w1_ref[...])
        ga = jnp.concatenate([dot_nt(up_ref[at, :], w2_ref[:, second]) for second in seconds], axis=1)
        square = h * h
        t = jnp.tanh(GELU_A * h * (1.0 + GELU_B * square))
        half = 0.5 + 0.5 * t
        act = (h * half).astype(LOW)
        slope = half + h * (0.5 - 0.5 * t * t) * (GELU_A + (3.0 * GELU_A * GELU_B) * square)
        gh = (ga * slope).astype(LOW)
        act_ref[at, :] = act
        gh_ref[at, :] = gh
        sum_ref[at, :] += sum(dot(act[:, first.start:first.start + first.size], w2_ref[:, second]) for first, second in zip(firsts, seconds))
        acc_ref[at, :] += dot_nt(gh, w1_ref[...])
    loop_rows(rows, rb, body)
    total = dot(nt_ref[...], gh_ref[...])
    if prior:
        total += old1_ref[...]
    dw1_ref[...] = total.astype(dw1_ref.dtype)
    for first, second in zip(firsts, seconds):
        total = dot_tn(act_ref[:, first], up_ref[...])
        if prior:
            total += old2_ref[:, second]
        dw2_ref[:, second] = total.astype(dw2_ref.dtype)

    @pl.when(step == steps - 1)
    def _():
        if prior:
            dgain_ref[...] = oldg_ref[...]
        else:
            dgain_ref[...] = jnp.zeros_like(dgain_ref)

        def last(group, k, at):
            out_pieces[k][group] = (keep_ref[at, :] * sum_ref[at, :]).astype(LOW)
            back, gains = norm_back(second_ref[at, :], gain_ref[...], acc_ref[at, :])
            dgain_ref[...] += gains
            grad_ref[at, :] = up_ref[at, :].astype(F32) + back
        each_span(last)


def whole(shape, at=None):
    spot = (0,) * len(shape) if at is None else at
    return pl.BlockSpec(shape, lambda i: spot, pipeline_mode=pl.Buffered(1))


def params():
    return pltpu.CompilerParams(dimension_semantics=("arbitrary",), vmem_limit_bytes=VMEM_LIMIT)


def spec_cols(shape, offset=0):
    return pl.BlockSpec(shape, lambda i, o=offset: (0, o + i))


def spec_rows(shape, column=0):
    return pl.BlockSpec(shape, lambda i: (i, column))


def weight_specs(width):
    quads = width // QUAD
    return [spec_cols((width, QUAD), at * quads) for at in range(3)] + [spec_rows((QUAD, width), 3)]


def piece_shapes(plan, width):
    return [jax.ShapeDtypeStruct((plan.groups, plan.span, width), LOW)] * plan.parts


def piece_specs(plan, width):
    return [whole((plan.groups, plan.span, width))] * plan.parts


def scalar():
    return pl.BlockSpec(memory_space=pltpu.SMEM)


LANES = 128


def gains_spec(bundle):
    rows, columns = bundle.shape
    return whole((rows, LANES), (0, columns // LANES - 1))


def run_attend_fwd(plan, space, micro, lead, gain, bias, weights):
    rows, width = plan.rows, gain.shape[0]
    tile = plan.slots if space else plan.tile_time
    quads = width // QUAD
    probs_rows = rows * 4
    low = jax.ShapeDtypeStruct((rows, width), LOW)
    cost = pl.CostEstimate(flops=rows * 4 // COST_SHARE * width * (4 * width + 8 * tile), bytes_accessed=rows * width, transcendentals=0)
    lead_specs = [scalar(), whole((1, rows, width), (micro, 0, 0))] if space else piece_specs(plan, width)
    out_specs = piece_specs(plan, width) if space else [whole((rows, width))]
    out_shape = piece_shapes(plan, width) if space else [jax.ShapeDtypeStruct((rows, width), F32)]
    result = pl.pallas_call(
        functools.partial(attend_fwd, plan, space),
        grid=(quads,),
        in_specs=lead_specs + [gains_spec(gain), whole(bias.shape)] + weight_specs(width),
        out_specs=out_specs + [whole((width, rows))] + [spec_cols((rows, QUAD))] * 3
        + [pl.BlockSpec((1, probs_rows, tile), lambda i: (i, 0, 0)), spec_cols((rows, QUAD))],
        out_shape=out_shape + [jax.ShapeDtypeStruct((width, rows), LOW), low, low, low,
                               jax.ShapeDtypeStruct((quads, probs_rows, tile), LOW), low],
        scratch_shapes=[pltpu.VMEM((rows, width), LOW), pltpu.VMEM((rows, width), F32), pltpu.VMEM((1, width), F32)],
        compiler_params=params(),
        cost_estimate=cost,
    )(*lead, gain, bias, weights, weights, weights, weights)
    return list(result[:len(out_shape)]), list(result[len(out_shape):])


def run_attend_bwd(plan, space, lead, gain, saved, weights, micro, micros, old=None, shared=None):
    rows, width = plan.rows, gain.shape[0]
    tile = plan.slots if space else plan.tile_time
    quads = width // QUAD
    probs_rows = rows * 4
    weight_type = LOW if micro == micros - 1 else F32
    cost = pl.CostEstimate(flops=rows * 4 // COST_SHARE * width * (8 * width + 20 * tile), bytes_accessed=rows * width, transcendentals=0)
    weight_out = [pl.BlockSpec((3, width, QUAD), lambda i: (0, 0, i)), spec_rows((QUAD, width)), whole((1, width))]
    token = whole((rows, width))
    deliver = space
    lead_specs = [scalar()] + piece_specs(plan, width) + [whole((1, rows, width), (micro, 0, 0))] + (piece_specs(plan, width) if deliver else []) if space else [token] + piece_specs(plan, width)
    if space:
        out_specs = [whole((1, rows, width), (micro, 0, 0))] * (1 + deliver)
        out_shape = [jax.ShapeDtypeStruct((micros, rows, width), kind) for kind in ((F32, LOW) if deliver else (F32,))]
    else:
        out_specs, out_shape = piece_specs(plan, width), piece_shapes(plan, width)
    operands = [*lead, gain, *saved, weights, weights, weights, weights]
    in_specs = (lead_specs + [gains_spec(gain), whole((width, rows))] + [spec_cols((rows, QUAD))] * 3
                + [pl.BlockSpec((1, probs_rows, tile), lambda i: (i, 0, 0)), spec_cols((rows, QUAD))] + weight_specs(width))
    if old is not None:
        operands += old
        in_specs = in_specs + weight_out
    aliases = {}
    if shared is not None:
        aliases = {len(operands): 0, len(operands) + 1: 1}
        operands += shared
        in_specs = in_specs + [pl.BlockSpec(memory_space=pl.ANY)] * 2
    result = pl.pallas_call(
        functools.partial(attend_bwd, plan, space, old is not None, shared is not None, deliver),
        grid=(quads,),
        in_specs=in_specs,
        out_specs=out_specs + weight_out,
        out_shape=out_shape + [jax.ShapeDtypeStruct((3, width, width), weight_type),
                               jax.ShapeDtypeStruct((width, width), weight_type), jax.ShapeDtypeStruct((1, width), F32)],
        scratch_shapes=[pltpu.VMEM((rows, width), LOW)] + [pltpu.VMEM((rows, QUAD), LOW)] * 4 + [pltpu.VMEM((rows, width), F32), pltpu.VMEM((1, width), F32)],
        input_output_aliases=aliases,
        compiler_params=params(),
        cost_estimate=cost,
    )(*operands)
    return list(result[:len(out_shape)]), list(result[len(out_shape):])


FF_TILE = 512
UNITS = 256


def run_mlp(plan, second, cots, keep, gain, weights, last, old=None):
    rows, width = second.shape
    hidden = weights.shape[1] // 2
    steps = hidden // FF_TILE
    joint = FF_TILE // UNITS
    blocks = width // UNITS
    weight_type = LOW if last else F32
    cost = pl.CostEstimate(flops=rows * 14 // COST_SHARE * width * hidden, bytes_accessed=rows * width, transcendentals=0)

    def second_spec(start):
        return pl.BlockSpec((UNITS, joint * width), lambda i: (i % blocks, start // (joint * width) + i // blocks))
    weight_out = [spec_cols((width, FF_TILE)), second_spec(0), whole((1, width))]
    token = whole((rows, width))
    result = pl.pallas_call(
        functools.partial(mlp_both, plan, old is not None),
        grid=(steps,),
        in_specs=[token] + piece_specs(plan, width) + [whole((rows, 1)), gains_spec(gain),
                  spec_cols((width, FF_TILE)), second_spec(hidden)] + ([] if old is None else weight_out),
        out_specs=piece_specs(plan, width) + [token] + weight_out,
        out_shape=piece_shapes(plan, width) + [jax.ShapeDtypeStruct((rows, width), F32),
                   jax.ShapeDtypeStruct((width, hidden), weight_type), jax.ShapeDtypeStruct((width, hidden), weight_type),
                   jax.ShapeDtypeStruct((1, width), F32)],
        scratch_shapes=[pltpu.VMEM((rows, width), LOW), pltpu.VMEM((width, rows), LOW), pltpu.VMEM((rows, width), LOW),
                        pltpu.VMEM((rows, width), F32),
                        pltpu.VMEM((rows, FF_TILE), LOW), pltpu.VMEM((rows, FF_TILE), LOW), pltpu.VMEM((1, width), F32)],
        compiler_params=params(),
        cost_estimate=cost,
    )(second, *cots, keep, gain, weights, weights, *([] if old is None else old))
    return list(result[:plan.parts]), result[plan.parts], list(result[plan.parts + 1:])


class Units:
    def __init__(self, devices, width, hidden):
        self.devices, self.rows = devices, width // devices
        self.ratio, self.joint = hidden // width, FF_TILE // UNITS
        self.blocks = width // UNITS

    def first_in(self, v):
        lead = v.shape[0]
        v = v.reshape(lead, self.devices, self.ratio, self.rows).transpose(0, 2, 1, 3)
        v = v.reshape(lead, self.ratio // self.joint, self.joint, self.blocks, UNITS).transpose(0, 1, 3, 2, 4)
        return v.reshape(lead, -1)

    def first_out(self, v):
        lead = v.shape[0]
        v = v.reshape(lead, self.ratio // self.joint, self.blocks, self.joint, UNITS).transpose(0, 1, 3, 2, 4)
        v = v.reshape(lead, self.ratio, self.devices, self.rows).transpose(0, 2, 1, 3)
        return v.reshape(lead, -1)

    def second_in(self, v):
        return v.reshape(self.ratio, self.rows, -1).transpose(1, 0, 2).reshape(self.rows, -1)

    def second_out(self, v):
        return v.reshape(self.rows, self.ratio, -1).transpose(1, 0, 2).reshape(self.rows * self.ratio, -1)


def swap(v, axis, size, by):
    return lax.ppermute(v, axis, [(i, i ^ by) for i in range(size)])


def exchange(pieces):
    return [piece if at == 0 else swap(piece, "seq", len(pieces), at) for at, piece in enumerate(pieces)]


def pick(v, at):
    return lax.dynamic_index_in_dim(v, at, 0, False)


def collect(v, axis, size, me, stride=1):
    count = size * stride
    out = jnp.zeros((size,) + v.shape, v.dtype)
    for at in range(size):
        out = lax.dynamic_update_index_in_dim(out, v if at == 0 else swap(v, axis, count, at * stride), lax.bitwise_xor(me, at), 0)
    return out


def reduce_blocks(v, axis, size, me, stride=1):
    count = size * stride
    parts = [swap(pick(v, lax.bitwise_xor(me, at)), axis, count, at * stride) for at in range(1, size)]
    total = pick(v, me).astype(F32)
    for part in parts:
        total += part.astype(F32)
    return total


def join_cores(v, dp):
    other = swap(v, "dp", dp, 1)
    core = (lax.axis_index("dp") % 2) == 0
    v = jnp.stack([jnp.where(core, v, other), jnp.where(core, other, v)], axis=1)
    return v.reshape(-1, v.shape[-1])


def scatter_rows(v, dp, seq):
    device, place = lax.axis_index("dp"), lax.axis_index("seq")
    rows, width = v.shape
    v = v.reshape(dp // 2, 2, rows // dp, width)
    core = device % 2
    own = lax.dynamic_index_in_dim(v, core, 1, False)
    got = swap(lax.dynamic_index_in_dim(v, 1 - core, 1, False), "dp", dp, 1)
    v = (own.astype(F32) + got.astype(F32)).astype(LOW)
    v = reduce_blocks(v, "dp", dp // 2, device // 2, 2).astype(LOW)
    return reduce_blocks(v.reshape(seq, rows // (dp * seq), width), "seq", seq, place)


def shards(dp, seq, frames_in, qkv_spatial, out_spatial, qkv_temporal, out_temporal, mlp_in, mlp_out, gains, place_mask, cotangent):
    micros, clips, local_frames, slots, width = frames_in.shape
    hidden = mlp_in.shape[1]
    plan = Plan(seq, clips, local_frames, slots)
    place = lax.axis_index("seq")
    me = place.astype(jnp.int32).reshape(1)

    units = Units(dp * seq, width, hidden)
    after = lax.optimization_barrier

    def cot_pieces(v):
        v = plan.fill(v).transpose(0, 2, 1, 3, 4).reshape(seq, local_frames, plan.groups, plan.group, width)
        return [pick(v, lax.bitwise_xor(place, at)).transpose(1, 0, 2, 3).reshape(plan.groups, plan.span, width) for at in range(seq)]

    padded_gains = jnp.pad(gains, ((0, 0), (0, LANES - gains.shape[1])))
    space = jnp.concatenate([qkv_spatial, out_spatial, padded_gains], axis=1)
    rest = jnp.concatenate([qkv_temporal, out_temporal, units.first_in(mlp_in), units.second_in(mlp_out)], axis=1)
    space, rest = after((space, rest))
    rest = lax.all_gather(rest, "seq", axis=0, tiled=True)
    cots = [exchange(cot_pieces(cotangent[0]))]
    space = collect(space, "seq", seq, place)
    device = lax.axis_index("dp")
    space = collect(space, "dp", dp // 2, device // 2, 2)
    space, cots[0][:EARLY] = after((space, cots[0][:EARLY]))
    space = join_cores(space, dp)
    bias_space = jnp.where(place_mask > 0, 0.0, -1000000000.0).astype(F32).reshape(plan.per_clip, plan.places)
    bias_space = jnp.pad(bias_space, ((0, 0), (0, plan.room - plan.places)), constant_values=-1000000000.0).reshape(1, plan.slots)
    spot = jnp.arange(plan.tile_time) % plan.group
    bias_time = jnp.where(spot[:, None] == spot[None, :], 0.0, -1000000000.0).astype(F32)
    bias_time = jnp.concatenate([bias_time, bias_time], axis=0)
    keep = pick(place_mask.astype(F32).reshape(plan.per_clip, plan.places), place % plan.per_clip)
    keep = jnp.pad(keep, (0, plan.room - plan.places)).reshape(plan.groups, 1, plan.group)
    keep = jnp.broadcast_to(keep, (plan.groups, seq * local_frames, plan.group)).reshape(plan.rows, 1)

    inputs = plan.fill_all(frames_in).reshape(micros, plan.rows, width)
    space_saved, across = [], []
    for m in range(micros):
        out, saved = run_attend_fwd(plan, True, m, [me, inputs], space, bias_space, space)
        space_saved.append(saved)
        across.append(exchange(out))
        if m == 0:
            rest, _ = after((rest, out[0]))
            time = lax.all_gather(rest[:, :4 * width], "dp", axis=0, tiled=True)
            mlp = lax.all_gather(rest[:, 4 * width:], "dp", axis=0, tiled=True)
            me, cots[0] = after((me, cots[0]))

    def scatter(parts):
        v = lax.psum_scatter(parts, "dp", scatter_dimension=0, tiled=True)
        return reduce_blocks(v.reshape(seq, v.shape[0] // seq, -1), "seq", seq, place)

    def attend_parts(old):
        return [old[0][0], old[0][1], old[0][2], old[1]]

    done, afters, time_saved, grads = [], [], [], []
    old_mlp = old_time = old_space = shared = None
    outs = []
    for m in range(micros):
        (second,), saved = run_attend_fwd(plan, False, m, across[m], space, bias_time, time)
        time_saved.append(saved)
        if m > 0:
            second, outs[m - 1] = after((second, outs[m - 1]))
            done.append(exchange(outs[m - 1]))
        if m + 1 < micros:
            second, across[m + 1], cot = after((second, across[m + 1], cotangent[m + 1]))
            cots.append(exchange(cot_pieces(cot)))
        out, grad, old_mlp = run_mlp(plan, second, cots[m], keep, space, mlp, m == micros - 1, old_mlp)
        outs.append(out)
        grads.append(grad)
        if m + 1 < micros:
            across[m + 1], cots[m + 1], old_mlp[2] = after((across[m + 1], cots[m + 1], old_mlp[2]))
    old_mlp, done = after((old_mlp, done))
    bundle = jnp.concatenate(old_mlp[:2], axis=1)
    grads[0], bundle = after((grads[0], bundle))
    owned_mlp = scatter(bundle)
    for m in range(micros):
        grads[m], old_mlp[2], done = after((grads[m], old_mlp[2], done))
        if m == 0:
            done.append(exchange(outs[-1]))
        back, old_time = run_attend_bwd(plan, False, [grads[m], *across[m]], space, time_saved[m], time, m, micros, old_time)
        afters.append(exchange(back))
    old_time, afters[0] = after((old_time, afters[0]))
    owned_time = scatter(jnp.concatenate(attend_parts(old_time), axis=1))
    for m in range(micros):
        if m == micros - 1:
            afters[m], owned_mlp = after((afters[m], owned_mlp))
        shared, old_space = run_attend_bwd(plan, True, [me, *afters[m], inputs, *done[m]], space, space_saved[m], space, m, micros, old_space, shared)
    old_space, owned_time = after((old_space, owned_time))

    gain_grads = jnp.concatenate([old_space[2], old_time[2], old_mlp[2]], axis=0).T.astype(LOW)
    owned = scatter_rows(jnp.concatenate(attend_parts(old_space) + [jnp.pad(gain_grads, ((0, 0), (0, LANES - gain_grads.shape[1])))], axis=1), dp, seq)
    return (
        plan.strip(shared[1], (micros, clips)),
        plan.strip(shared[0], (micros, clips)),
        owned[:, :3 * width],
        owned[:, 3 * width:4 * width],
        owned_time[:, :3 * width],
        owned_time[:, 3 * width:],
        units.first_out(owned_mlp[:, :hidden]),
        units.second_out(owned_mlp[:, hidden:]),
        owned[:, 4 * width:4 * width + gains.shape[1]],
    )


def solution(mesh):
    rows = P(("dp", "seq"), None)
    tokens = P(None, "dp", "seq", None, None)
    return jax.shard_map(
        functools.partial(shards, mesh.shape["dp"], mesh.shape["seq"]),
        mesh=mesh,
        in_specs=(tokens,) + (rows,) * 7 + (P(), tokens),
        out_specs=(tokens, tokens) + (rows,) * 7,
        check_vma=False,
    )
```
